32 devices in a mesh: member: 2 (over y), lon: 4 (over z), lat: 4 (over x, core).
Axes of the slice: x: 2, y: 2, z: 4, core: 2. Of those that a mesh axis runs over, the one named last changes fastest.
Arguments:
- tracer: float32 [20, 16, 64, 512], P('member', None, 'lat', 'lon'), parts along dimension 0, may hold values from -6 to 6
- ocean_mask: int32 [64, 512], P('lat', 'lon'), may hold values 0 or 1
- diffusivity: float32 [64, 512], P('lat', 'lon'), may hold values from 0.12 to 0.24
- remap_cell: int32 [2048, 128], P(('lon', 'lat')), may hold values from 0 to 2047
- remap_column: int32 [2048, 128], P(('lon', 'lat')), may hold values from 0 to 255
- remap_weight: float32 [2048, 128], P(('lon', 'lat')), may hold values from 0.05 to 0.2
- remap_owner: int32 [2048, 1], P(('lon', 'lat')), may hold values from 0 to 15; in each aligned block of 128 rows (0 to 127, 128 to 255, ...) at most 21 rows name the same one
Outputs:
- updated: float32 [20, 16, 64, 512], P('member', None, 'lat', 'lon'), parts along dimension 0
- atmosphere: float32 [20, 4096], P('member', ('lon', 'lat')), parts along dimension 0
The draws below stay inside these ranges and needn't reach their ends.
There are 2 independent parts, one for each index of `member`. The reference program is written for one: setup_inputs(seed, part) draws one part's arguments, and reference() takes and returns one part's arrays. A program takes and returns all parts, laid end to end along the dimension named above; an argument that names none is the same for every part. Nothing has to cross between parts.
Inputs may be any that keep to these rules, and one draw needn't show every extreme that they name: `remap_owner`: among the 128 blocks of one device at most 21 have the same owner.
All inputs are finite; a program needn't handle non-finite values. No bound on the sum of `ocean_mask` on one device may be relied on, other than what follows from the above.
Results may differ from the reference program's by a relative error of at most 0.000082.
Values sent between devices are 32-bit elements; how exact they have to be, the bound alone decides.
No kernel may reach another device: no remote copies, remote signals or barrier semaphores. Data moves between devices by JAX's collectives and lax.ppermute only.
A program may use at most 64 MiB of HBM per device.

```python
import math
import jax
import jax.numpy as jnp
import numpy as np

NTR = 10
LEV = 16
CLAT = 16
CLON = 128
ACOL = 256
ENTRY = 128
SUBSTEPS = 3
NY = 64
NX = 512
OWNERS = 16
NBLK = 128
BLOCKS = 2048
CAP = 21
N_LAT = 4


def with_ends(entries, stream_key, low, largest):
    dims = entries.shape
    spot = [jax.random.randint(jax.random.fold_in(stream_key, axis), (), 0, dims[axis]) for axis in range(len(dims))]
    entries = entries.at[tuple(spot)].set(low)
    longest = dims.index(max(dims))
    spot[longest] = (spot[longest] + 1) % dims[longest]
    return entries.at[tuple(spot)].set(largest)


def block_scale(stream_key, shape, pieces, low, largest):
    def one(axis_at, shards_of):
        heights = jax.random.uniform(jax.random.fold_in(jax.random.fold_in(stream_key, 6), axis_at), (shards_of,), jnp.float32, low / len(pieces), largest / len(pieces))
        return jnp.repeat(jnp.exp(heights), shape[axis_at] // shards_of).reshape((-1,) + (1,) * (len(shape) - axis_at - 1))

    factor_of = one(*pieces[0])
    for cut in pieces[1:]:
        factor_of = factor_of * one(*cut)
    return factor_of


def assign_block(rng, own, number, rows, number_of, top, limit, lean):
    sequence = jax.random.permutation(rng, number_of)
    packed, usual = shares(number_of, rows * top, limit, lean, True), shares(number_of, rows * top, limit, lean, False)
    places = jnp.arange(number_of)

    def named(lengths, offset_by):
        used = int((lengths > 0).sum())
        fixed = max(1, used // 4)
        passed = fixed + (places - fixed + offset_by * (used - fixed)) % max(1, number_of - fixed)
        return jnp.zeros((number_of,), jnp.int32).at[sequence[jnp.where(places < fixed, places, passed)]].set(jnp.asarray(lengths, jnp.int32))

    lengths = jnp.where(number % 4 == 0, named(packed, number // 4), named(usual, number - number // 4 - 1))
    mixed = jax.random.permutation(jax.random.fold_in(own, 3), number_of)
    giver, sink = mixed[0:number_of // 2 * 2:2], mixed[1:number_of // 2 * 2:2]
    slack = jnp.minimum(lengths[giver] - 1, limit - lengths[sink]) // 2
    slack = jnp.where((giver == sequence[0]) | (sink == sequence[0]) | (lengths[sink] == 0), 0, jnp.maximum(slack, 0))
    passed = jax.random.randint(jax.random.fold_in(own, 4), (number_of // 2,), 0, 1 << 20) % (slack + 1)
    lengths = lengths.at[giver].add(-passed).at[sink].add(passed)
    labels = jnp.searchsorted(jnp.cumsum(lengths), jnp.arange(rows * top), side="right").astype(jnp.int32)
    listing = labels.reshape(top, rows).T
    listing = listing[jax.random.permutation(jax.random.fold_in(own, 1), rows)]
    offset_by = jax.random.randint(jax.random.fold_in(own, 2), (rows, 1), 0, top)
    return jnp.take_along_axis(listing, (jnp.arange(top)[None, :] + offset_by) % top, axis=1)


def shares(number_of, total, limit, lean, full):
    loads = [(1 << 20) // math.isqrt(standing ** lean) + 1 for standing in range(1, number_of + 1)]
    largest = limit if full else min(limit, max(-(-total // number_of), total * loads[0] // sum(loads)))
    least = 1 if total - largest >= number_of - 1 else 0
    holding, surplus = [largest] + [least] * (number_of - 1), total - largest - least * (number_of - 1)
    while surplus > 0:
        movable = [i for i in range(1, number_of) if holding[i] < largest] or [i for i in range(1, number_of) if holding[i] < limit]
        whole, budget = sum([loads[i] for i in movable]), surplus
        for i in movable:
            more = min(limit - holding[i], max(1, budget * loads[i] // whole), surplus)
            holding[i] = holding[i] + more
            surplus = surplus - more
    return np.array(holding)


def noise(key, dims, scale, limit, pieces=(), held_as=jnp.bfloat16):
    level = block_scale(key, dims, pieces, -0.22, 0.18) if pieces else 1.0
    values = jax.random.normal(key, dims, jnp.float32) * scale * level
    return jnp.minimum(jnp.maximum(values, -limit), limit).astype(held_as)


def setup_inputs(seed: int = 0, part: int = 0) -> dict:
    arg_keys = jax.random.split(jax.random.key(seed), 8)
    part_splits = jax.random.split(jax.random.fold_in(arg_keys[7], part), 8)
    tracer = noise(part_splits[0], (NTR, LEV, NY, NX), 1.0, 6.0, ((2, 4), (3, 4)), jnp.float32)
    ocean_mask = with_ends((jax.random.randint(arg_keys[1], (NY, NX), 0, 4) < 3).astype(jnp.int32), jax.random.fold_in(arg_keys[1], 1), 0, 1)
    diffusivity = jnp.clip(jnp.exp(math.log(0.24) - 0.6931472 * jax.random.uniform(arg_keys[2], (NY, NX), jnp.float32) ** block_scale(arg_keys[2], (NY, NX), ((0, 4), (1, 4)), -0.2, 0.2)), 0.12, 0.24)
    remap_cell = with_ends(jax.random.randint(arg_keys[3], (BLOCKS, ENTRY), 0, CLAT * CLON), jax.random.fold_in(arg_keys[3], 1), 0, (CLAT * CLON) - 1).astype(jnp.int32)
    remap_column = with_ends(jax.random.randint(arg_keys[4], (BLOCKS, ENTRY), 0, ACOL), jax.random.fold_in(arg_keys[4], 1), 0, ACOL - 1).astype(jnp.int32)
    remap_weight = jnp.clip(0.05 + 0.15 * jax.random.uniform(arg_keys[5], (BLOCKS, ENTRY), jnp.float32) ** block_scale(arg_keys[5], (BLOCKS, ENTRY), ((0, 16),), -0.2, 0.2), 0.05, 0.2)
    remap_owner_keys = jax.random.split(jax.random.fold_in(arg_keys[6], 1), BLOCKS // NBLK)
    remap_owner_turns = jax.random.permutation(jax.random.fold_in(arg_keys[6], 3), BLOCKS // NBLK)
    remap_owner = jax.vmap(lambda own, number: assign_block(jax.random.fold_in(arg_keys[6], 2), own, number, NBLK, OWNERS, 1, CAP, 2))(remap_owner_keys, remap_owner_turns).reshape((BLOCKS, 1))
    return dict(tracer=tracer, ocean_mask=ocean_mask, diffusivity=diffusivity, remap_cell=remap_cell, remap_column=remap_column, remap_weight=remap_weight, remap_owner=remap_owner)


neighbour_offsets = ((1, 0), (-1, 0), (0, 1), (0, -1))


def neighbour(array, shift_row, shift_col):
    height = array.shape[-2] - 2
    breadth = array.shape[-1] - 2
    return array[..., 1 + shift_row:1 + shift_row + height, 1 + shift_col:1 + shift_col + breadth]


def relax(extended):
    wetness = extended[-2]
    spread = extended[-1]
    fields = extended[:-2]
    centre_wet = wetness[1:-1, 1:-1]
    centre_diff = spread[1:-1, 1:-1]
    centre = fields[:, 1:-1, 1:-1]
    change = jnp.zeros_like(centre)
    for shift_row, shift_col in neighbour_offsets:
        beside_wet = neighbour(wetness, shift_row, shift_col)
        beside_diff = neighbour(spread, shift_row, shift_col)
        beside = neighbour(fields, shift_row, shift_col)
        coupling = 0.5 * (centre_diff + beside_diff) * centre_wet * beside_wet
        change = change + coupling * (beside - centre)
    return jnp.concatenate([centre + change, centre_wet[None], centre_diff[None]], axis=0)


def pad_once(fields_stack):
    northern = jnp.flip(fields_stack[:, -1:, :], axis=(1, 2))
    southern = jnp.zeros_like(fields_stack[:, :1, :])
    extended_rows = jnp.concatenate([southern, fields_stack, northern], axis=1)
    return jnp.concatenate([extended_rows[:, :, -1:], extended_rows, extended_rows[:, :, :1]], axis=2)


def reference(tracer, ocean_mask, diffusivity, remap_cell, remap_column, remap_weight, remap_owner):
    wetness = ocean_mask.astype(jnp.float32)
    fields_stack = jnp.concatenate([tracer.reshape(NTR * LEV, NY, NX), wetness[None], diffusivity[None]], axis=0)
    for substep in range(SUBSTEPS):
        fields_stack = relax(pad_once(fields_stack))
    updated = fields_stack[:-2].reshape(NTR, LEV, NY, NX)
    surface = tracer[:, 0]
    device = (jnp.arange(NBLK * OWNERS) // NBLK).astype(jnp.int32)
    lon_index = device // N_LAT
    lat_index = device % N_LAT
    global_row = lat_index[:, None] * CLAT + remap_cell // CLON
    global_col = lon_index[:, None] * CLON + remap_cell % CLON
    picked = surface[:, global_row, global_col] * remap_weight[None]
    targets = remap_owner[:, 0:1] * ACOL + remap_column
    atmosphere = jax.ops.segment_sum(picked.reshape(NTR, -1).T, targets.reshape(-1), num_segments=ACOL * OWNERS).T
    return updated, atmosphere
```

```python
import functools

import jax
import jax.numpy as jnp
from jax import lax
from jax.experimental import pallas as pl
from jax.experimental.pallas import tpu as pltpu
from jax.sharding import PartitionSpec as P

ACOL = 256
SUBSTEPS = 3
LANES = 128
GROUP = 8
EDGE = 6
F32 = jnp.float32


def lane_iota(rows=GROUP):
    return lax.broadcasted_iota(jnp.int32, (rows, LANES), 1)


def edge_lane(row):
    return EDGE * (row + 2) + 2


def edge_pattern():
    place = lane_iota() % EDGE
    return jnp.where(place < 3, 2 - place, LANES + 2 - place)


def in_row(row):
    lane = lane_iota()
    return (lane >= EDGE * (row + 2)) & (lane < EDGE * (row + 3))


def take_lanes(value, index):
    return jnp.take_along_axis(value, index, axis=1)


def pack_kernel(height, chunks, info_ref, tracer_ref, mask_ref, diff_ref, a_ref, b_ref, m_ref):
    odd = info_ref[0]
    top = info_ref[1]
    lane = lane_iota()
    flip = jnp.where(jnp.full(lane.shape, top) == 1, LANES - 1 - lane, lane)
    pattern = edge_pattern()

    def near(d):
        return jnp.where(odd == 1, height - 1 - d, d)

    def one(c, unused):
        base = c * (GROUP * height)
        edges = jnp.zeros((GROUP, LANES), F32)
        for row in range(height):
            value = tracer_ref[pl.ds(base + row, GROUP, stride=height), :]
            edges = jnp.where(in_row(row), take_lanes(value, pattern), edges)
        m_ref[pl.ds(c * GROUP, GROUP), :] = edges
        for d in range(SUBSTEPS):
            first = tracer_ref[pl.ds(base + near(d), GROUP, stride=height), :]
            a_ref[d, pl.ds(c * GROUP, GROUP), :] = take_lanes(first, flip)
            b_ref[d, pl.ds(c * GROUP, GROUP), :] = tracer_ref[
                pl.ds(base + height - 1 - near(d), GROUP, stride=height), :
            ]
        return unused

    lax.fori_loop(0, chunks, one, 0)

    sub = lax.broadcasted_iota(jnp.int32, (GROUP, LANES), 0)

    def fixed(row):
        wet = jnp.broadcast_to(mask_ref[pl.ds(row, 1), :].astype(F32), (GROUP, LANES))
        spread = jnp.broadcast_to(diff_ref[pl.ds(row, 1), :], (GROUP, LANES))
        return jnp.where(sub == 0, wet, jnp.where(sub == 1, spread, 0.0))

    last = pl.ds(chunks * GROUP, GROUP)
    edges = jnp.zeros((GROUP, LANES), F32)
    for row in range(height):
        edges = jnp.where(in_row(row), take_lanes(fixed(row), pattern), edges)
    m_ref[last, :] = edges
    m_ref[pl.ds((chunks + 1) * GROUP, GROUP), :] = jnp.zeros((GROUP, LANES), F32)
    for d in range(SUBSTEPS):
        a_ref[d, last, :] = take_lanes(fixed(near(d)), flip)
        b_ref[d, last, :] = fixed(height - 1 - near(d))


def pick_rows(odd, a_ref, b_ref, d, rows):
    first = a_ref[d, rows, :]
    second = b_ref[d, rows, :]
    swap = jnp.full(first.shape, odd) == 1
    return jnp.where(swap, first, second), jnp.where(swap, second, first)


def columns_kernel(height, chunks, info_ref, a_ref, b_ref, m_ref, east_ref, west_ref):
    odd = info_ref[0]
    pattern = edge_pattern()
    to_west = lane_iota() % EDGE < 3

    def extended(c):
        rows = pl.ds(c * GROUP, GROUP)
        edges = m_ref[rows, :]
        for d in range(SUBSTEPS - 1):
            north, south = pick_rows(odd, a_ref, b_ref, d, rows)
            edges = jnp.where(in_row(height + d), take_lanes(north, pattern), edges)
            edges = jnp.where(in_row(-1 - d), take_lanes(south, pattern), edges)
        return edges

    def put(i, first, second):
        rows = pl.ds(i * GROUP, GROUP)
        west_ref[rows, :] = jnp.where(to_west, first, pltpu.roll(second, 3, 1))
        east_ref[rows, :] = jnp.where(to_west, pltpu.roll(second, LANES - 3, 1), first)

    def one(i, unused):
        put(i, extended(2 * i), extended(2 * i + 1))
        return unused

    lax.fori_loop(0, chunks // 2, one, 0)
    put(chunks // 2, extended(chunks), m_ref[pl.ds((chunks + 1) * GROUP, GROUP), :])


def stencil_kernel(
    height,
    info_ref,
    tracer_ref,
    mask_ref,
    diff_ref,
    a_ref,
    b_ref,
    fe_ref,
    fw_ref,
    out_ref,
    coef,
    edge_coef,
):
    odd = info_ref[0]
    step = pl.program_id(0)
    chunks_all = pl.num_programs(0) * 2
    lane = lane_iota()
    to_east = lane % EDGE < 3
    is_e0 = lane % EDGE == 2
    is_w2 = lane % EDGE == 3
    low, high = -2, height + 2

    def pull(edges, row):
        return pltpu.roll(edges, (LANES - (edge_lane(row) + 1)) % LANES, 1)

    def sides(value, edges, row):
        beyond = pull(edges, row)
        east = jnp.where(lane == LANES - 1, beyond, pltpu.roll(value, LANES - 1, 1))
        west = jnp.where(lane == 0, beyond, pltpu.roll(value, 1, 1))
        return east, west

    def inner(values, rows):
        found = jnp.zeros((GROUP, LANES), F32)
        for row in rows:
            found = jnp.where(in_row(row), pltpu.roll(values[row], edge_lane(row) + 1, 1), found)
        return found

    def edge_neighbours(edges, found):
        right = jnp.where(is_e0, found, pltpu.roll(edges, LANES - 1, 1))
        left = jnp.where(is_w2, found, pltpu.roll(edges, 1, 1))
        return (
            right,
            left,
            pltpu.roll(edges, LANES - EDGE, 1),
            pltpu.roll(edges, EDGE, 1),
        )

    @pl.when(step == 0)
    def prepare():
        rows = pl.ds(chunks_all * GROUP, GROUP)
        wet, spread = {}, {}

        def spread_out(value):
            return (
                jnp.broadcast_to(value[0:1, :], (GROUP, LANES)),
                jnp.broadcast_to(value[1:2, :], (GROUP, LANES)),
            )

        for row in range(height):
            wet[row] = jnp.broadcast_to(mask_ref[row : row + 1, :].astype(F32), (GROUP, LANES))
            spread[row] = jnp.broadcast_to(diff_ref[row : row + 1, :], (GROUP, LANES))
        for d in range(SUBSTEPS):
            north, south = pick_rows(odd, a_ref, b_ref, d, rows)
            wet[height + d], spread[height + d] = spread_out(north)
            wet[-1 - d], spread[-1 - d] = spread_out(south)
        half = pl.ds((chunks_all // 2) * GROUP, GROUP)
        edge_wet, edge_spread = spread_out(jnp.where(to_east, fe_ref[half, :], fw_ref[half, :]))

        def coupling(m, s, m_n, s_n):
            return 0.5 * (s + s_n) * m * m_n

        for row in range(low, high):
            m, s = wet[row], spread[row]
            m_e, m_w = sides(m, edge_wet, row)
            s_e, s_w = sides(s, edge_spread, row)
            north = coupling(m, s, wet[row + 1], spread[row + 1])
            south = coupling(m, s, wet[row - 1], spread[row - 1])
            east = coupling(m, s, m_e, s_e)
            west = coupling(m, s, m_w, s_w)
            at = row - low
            coef[at, 0] = 1.0 - (north + south + east + west)
            coef[at, 1] = north
            coef[at, 2] = south
            coef[at, 3] = east
            coef[at, 4] = west
        span = range(-1, height + 1)
        m_n = edge_neighbours(edge_wet, inner(wet, span))
        s_n = edge_neighbours(edge_spread, inner(spread, span))
        total = jnp.zeros((GROUP, LANES), F32)
        for i in range(4):
            c = coupling(edge_wet, edge_spread, m_n[i], s_n[i])
            edge_coef[1 + i] = c
            total = total + c
        edge_coef[0] = 1.0 - total

    from_east = fe_ref[pl.ds(step * GROUP, GROUP), :]
    from_west = fw_ref[pl.ds(step * GROUP, GROUP), :]
    for part in range(2):
        rows = pl.ds((2 * step + part) * GROUP, GROUP)
        base = part * GROUP * height
        value = {
            row: tracer_ref[pl.ds(base + row, GROUP, stride=height), :] for row in range(height)
        }
        for d in range(SUBSTEPS):
            value[height + d], value[-1 - d] = pick_rows(odd, a_ref, b_ref, d, rows)
        if part == 0:
            edges = jnp.where(to_east, from_east, from_west)
        else:
            edges = jnp.where(
                to_east, pltpu.roll(from_east, LANES - 3, 1), pltpu.roll(from_west, 3, 1)
            )
        for s in range(SUBSTEPS):
            reach = SUBSTEPS - 1 - s
            fresh = {}
            for row in range(-reach, height + reach):
                at = row - low
                east, west = sides(value[row], edges, row)
                fresh[row] = (
                    coef[at, 0] * value[row]
                    + (coef[at, 1] * value[row + 1] + coef[at, 2] * value[row - 1])
                    + (coef[at, 3] * east + coef[at, 4] * west)
                )
            if reach:
                n = edge_neighbours(edges, inner(value, range(1 - reach, height + reach - 1)))
                edges = (
                    edge_coef[0] * edges
                    + (edge_coef[1] * n[0] + edge_coef[2] * n[1])
                    + (edge_coef[3] * n[2] + edge_coef[4] * n[3])
                )
            value = fresh
        for row in range(height):
            out_ref[pl.ds(base + row, GROUP, stride=height), :] = value[row]


def remap_kernel(tracers, height, owners, owner_ref, surface_ref, cell_ref, column_ref, weight_ref, out_ref, picked_ref, total_ref):
    pad = 2 * GROUP
    total_ref[...] = jnp.zeros_like(total_ref)
    column = lax.broadcasted_iota(jnp.int32, (ACOL, LANES), 0)

    def one(g, unused):
        rows = pl.ds(g * GROUP, GROUP)
        cell = cell_ref[rows, :]
        at_lane = cell % LANES
        at_row = cell // LANES
        found = [jnp.zeros((GROUP, LANES), F32)] * tracers
        for row in range(height):
            here = at_row == row
            for k in range(tracers):
                source = jnp.broadcast_to(surface_ref[k, row : row + 1, :], (GROUP, LANES))
                found[k] = jnp.where(here, take_lanes(source, at_lane), found[k])
        weight = weight_ref[rows, :]
        for k in range(tracers):
            picked_ref[pl.ds(g * (GROUP * pad) + k, GROUP, stride=pad), :] = found[k] * weight
        for j in range(GROUP):
            block = g * GROUP + j
            value = picked_ref[pl.ds(block * pad, pad), :]
            coarse = value.astype(jnp.bfloat16)
            fine = (value - coarse.astype(F32)).astype(jnp.bfloat16)
            chosen = (column == column_ref[pl.ds(block, 1), :]).astype(F32).astype(jnp.bfloat16)
            product = lax.dot_general(
                jnp.concatenate([coarse, fine], axis=0),
                chosen,
                (((1,), (1,)), ((), ())),
                preferred_element_type=F32,
            )
            owner = owner_ref[block]
            total_ref[owner] = total_ref[owner] + (product[:pad] + product[pad:])
        return unused

    lax.fori_loop(0, cell_ref.shape[0] // GROUP, one, 0)

    def write(o, unused):
        for half in range(ACOL // LANES):
            out_ref[o, pl.ds(half * tracers, tracers), :] = total_ref[
                o, pl.ds(0, tracers), pl.ds(half * LANES, LANES)
            ]
        return unused

    lax.fori_loop(0, owners, write, 0)


def sum_kernel(tracers, parts_ref, out_ref):
    total = jnp.sum(parts_ref[...], axis=0)
    for half in range(ACOL // LANES):
        out_ref[:, half * LANES : (half + 1) * LANES] = total[half * tracers : (half + 1) * tracers]


def routes(lon, lat):
    def device(i, j):
        return i * lat + j

    def swaps(first, stop):
        found = []
        for i in range(lon):
            for j in range(first, stop, 2):
                found += [(device(i, j), device(i, j + 1)), (device(i, j + 1), device(i, j))]
        return found

    fold = [(device(i, lat - 1), device(lon - 1 - i, lat - 1)) for i in range(lon)]
    east = [(device(i, j), device((i + 1) % lon, j)) for i in range(lon) for j in range(lat)]
    west = [(b, a) for a, b in east]
    return swaps(1, lat - 1) + fold, swaps(0, lat), east, west


def whole():
    return pl.BlockSpec(memory_space=pltpu.VMEM)


def scalars():
    return pl.BlockSpec(memory_space=pltpu.SMEM)


def on_device(lon, lat, tracer, ocean_mask, diffusivity, remap_cell, remap_column, remap_weight, remap_owner):
    tracers, levels, height, breadth = tracer.shape
    layers = tracers * levels
    chunks = layers // GROUP
    owners = lon * lat
    both = ("lon", "lat")
    route_a, route_b, route_east, route_west = routes(lon, lat)
    lat_index = lax.axis_index("lat")
    info = jnp.stack([lat_index % 2, (lat_index == lat - 1).astype(jnp.int32)]).astype(jnp.int32)
    flat = tracer.reshape(layers * height, breadth)
    shape = jax.ShapeDtypeStruct
    rows = layers + 2 * GROUP

    with jax.named_scope("pack"):
        send_a, send_b, edges = pl.pallas_call(
            functools.partial(pack_kernel, height, chunks),
            out_shape=(
                shape((SUBSTEPS, rows - GROUP, LANES), F32),
                shape((SUBSTEPS, rows - GROUP, LANES), F32),
                shape((rows, LANES), F32),
            ),
            in_specs=[scalars(), whole(), whole(), whole()],
            out_specs=(whole(), whole(), whole()),
        )(info, flat, ocean_mask, diffusivity)
    got_a = lax.ppermute(send_a, both, route_a)
    got_b = lax.ppermute(send_b, both, route_b)

    with jax.named_scope("remap"):
        partial = pl.pallas_call(
            functools.partial(remap_kernel, tracers, height, owners),
            out_shape=shape((owners, tracers * ACOL // LANES, LANES), F32),
            grid=(1,),
            in_specs=[
                scalars(),
                pl.BlockSpec((tracers, height, LANES), lambda i: (0, 0, 0)),
                whole(),
                whole(),
                whole(),
            ],
            out_specs=whole(),
            scratch_shapes=[
                pltpu.VMEM((remap_cell.shape[0] * 2 * GROUP, LANES), F32),
                pltpu.VMEM((owners, 2 * GROUP, ACOL), F32),
            ],
        )(
            remap_owner.reshape(-1),
            tracer.reshape(tracers, levels * height, breadth),
            remap_cell,
            remap_column,
            remap_weight,
        )
    parts = lax.all_to_all(partial, both, 0, 0, tiled=True)

    with jax.named_scope("columns"):
        send_east, send_west = pl.pallas_call(
            functools.partial(columns_kernel, height, chunks),
            out_shape=(shape((rows // 2, LANES), F32), shape((rows // 2, LANES), F32)),
            in_specs=[scalars(), whole(), whole(), whole()],
            out_specs=(whole(), whole()),
        )(info, got_a, got_b, edges)
    from_west = lax.ppermute(send_east, both, route_east)
    from_east = lax.ppermute(send_west, both, route_west)

    block = pl.BlockSpec((levels * height, LANES), lambda i: (i, 0))
    with jax.named_scope("stencil"):
        updated = pl.pallas_call(
            functools.partial(stencil_kernel, height),
            out_shape=shape(flat.shape, F32),
            grid=(tracers,),
            in_specs=[scalars(), block, whole(), whole(), whole(), whole(), whole(), whole()],
            out_specs=block,
            scratch_shapes=[
                pltpu.VMEM((height + 4, 5, GROUP, LANES), F32),
                pltpu.VMEM((5, GROUP, LANES), F32),
            ],
        )(info, flat, ocean_mask, diffusivity, got_a, got_b, from_east, from_west)

    with jax.named_scope("sum"):
        atmosphere = pl.pallas_call(
            functools.partial(sum_kernel, tracers),
            out_shape=shape((tracers, ACOL), F32),
            in_specs=[whole()],
            out_specs=whole(),
        )(parts)
    return updated.reshape(tracer.shape), atmosphere


def solution(mesh):
    in_specs = (
        P("member", None, "lat", "lon"),
        P("lat", "lon"),
        P("lat", "lon"),
        P(("lon", "lat"), None),
        P(("lon", "lat"), None),
        P(("lon", "lat"), None),
        P(("lon", "lat"), None),
    )
    out_specs = (P("member", None, "lat", "lon"), P("member", ("lon", "lat")))
    return jax.shard_map(
        functools.partial(on_device, mesh.shape["lon"], mesh.shape["lat"]),
        mesh=mesh,
        in_specs=in_specs,
        out_specs=out_specs,
        check_vma=False,
    )
```

```python
import functools

import jax
import jax.numpy as jnp
from jax import lax
from jax.experimental import pallas as pl
from jax.experimental.pallas import tpu as pltpu
from jax.sharding import PartitionSpec as P

ACOL = 256
SUBSTEPS = 3
LANES = 128
GROUP = 8
F32 = jnp.float32

STRIP = 18
PER = 7
SETS = 3
HALF = 6


def lane_iota():
    return lax.broadcasted_iota(jnp.int32, (GROUP, LANES), 1)


def shift(value, amount):
    amount = amount % LANES
    return pltpu.roll(value, amount, 1) if amount else value


def take_lanes(value, index):
    return jnp.take_along_axis(value, index, axis=1)


def is_odd():
    return lax.axis_index("lat") % 2


def base_of(chunk):
    return chunk // PER, STRIP * (chunk % PER)


def message_rows(layers):
    return SUBSTEPS * (layers + GROUP), SUBSTEPS * (layers + GROUP) + SUBSTEPS * SETS * GROUP


def pack_kernel(
    height,
    chunks,
    parts,
    tracer_ref,
    mask_ref,
    diff_ref,
    a_ref,
    b_ref,
    p_ref,
    x_ref,
    tile,
    wet_tile,
    spread_tile,
    sems,
):
    odd = jnp.full((GROUP, LANES), is_odd()) == 1
    top = (lax.axis_index("lat") == lax.axis_size("lat") - 1).astype(jnp.int32)
    each = chunks // parts
    size = each * GROUP * height
    copies = [
        pltpu.make_async_copy(
            tracer_ref.at[pl.ds(p * size, size)], tile.at[pl.ds(p * size, size)], sems.at[p]
        )
        for p in range(parts)
    ]
    copies.append(pltpu.make_async_copy(mask_ref, wet_tile, sems.at[parts]))
    copies.append(pltpu.make_async_copy(diff_ref, spread_tile, sems.at[parts + 1]))
    for copy in copies:
        copy.start()

    lane = lane_iota()
    place = lane % STRIP
    is_top = jnp.full((GROUP, LANES), top) == 1
    flip = jnp.where(is_top, LANES - 1 - lane, lane)
    flip_strip = jnp.where(is_top & (place < 2 * HALF), lane - place + 2 * HALF - 1 - place, lane)
    stride = (chunks + 1) * GROUP
    strips_at = SUBSTEPS * stride

    def send(c, value):
        for d in range(SUBSTEPS):
            rows = pl.ds(d * stride + c * GROUP, GROUP)
            near, far = value[d], value[height - 1 - d]
            a_ref[rows, :] = take_lanes(jnp.where(odd, far, near), flip)
            b_ref[rows, :] = jnp.where(odd, near, far)

    strips = {}

    def edge(c, value):
        which, base = base_of(c)
        here = (lane >= base) & (lane < base + 2 * HALF)
        for row in range(height):
            before = strips.get((row, which), jnp.zeros((GROUP, LANES), F32))
            strips[row, which] = jnp.where(here, shift(value[row], base + HALF), before)

    for p in range(parts):
        copies[p].wait()
        for c in range(p * each, (p + 1) * each):
            value = {}
            for row in range(height):
                value[row] = tile[pl.ds(c * GROUP * height + row, GROUP, stride=height), :]
                x_ref[row, pl.ds(c * GROUP, GROUP), :] = value[row]
            send(c, value)
            edge(c, value)

    copies[parts].wait()
    copies[parts + 1].wait()
    sub = lax.broadcasted_iota(jnp.int32, (GROUP, LANES), 0)
    value = {}
    for row in range(height):
        wet = jnp.broadcast_to(wet_tile[row : row + 1, :].astype(F32), (GROUP, LANES))
        spread = jnp.broadcast_to(spread_tile[row : row + 1, :], (GROUP, LANES))
        value[row] = jnp.where(sub == 0, wet, jnp.where(sub == 1, spread, 0.0))
    send(chunks, value)
    edge(chunks, value)

    zero = jnp.zeros((GROUP, LANES), F32)
    for row in range(height):
        for g in range(SETS):
            p_ref[row, g] = strips.get((row, g), zero)
    for d in range(SUBSTEPS):
        for g in range(SETS):
            near, far = strips.get((d, g), zero), strips.get((height - 1 - d, g), zero)
            rows = pl.ds(strips_at + (d * SETS + g) * GROUP, GROUP)
            a_ref[rows, :] = take_lanes(jnp.where(odd, far, near), flip_strip)
            b_ref[rows, :] = jnp.where(odd, near, far)


def pick_rows(odd, a_ref, b_ref, rows):
    first = a_ref[rows, :]
    second = b_ref[rows, :]
    return jnp.where(odd, first, second), jnp.where(odd, second, first)


def own_strips(height, chunks, a_ref, b_ref, p_ref, depth):
    odd = jnp.full((GROUP, LANES), is_odd()) == 1
    strips_at = SUBSTEPS * (chunks + 1) * GROUP
    found = {}
    for g in range(SETS):
        for row in range(height):
            found[row, g] = p_ref[row, g]
        for d in range(depth):
            rows = pl.ds(strips_at + (d * SETS + g) * GROUP, GROUP)
            found[height + d, g], found[-1 - d, g] = pick_rows(odd, a_ref, b_ref, rows)
    return found


def columns_kernel(height, chunks, a_ref, b_ref, p_ref, east_ref, west_ref):
    found = own_strips(height, chunks, a_ref, b_ref, p_ref, SUBSTEPS - 1)
    place = lane_iota() % STRIP
    rows = height + 2 * (SUBSTEPS - 1)
    for block in range(-(-rows // 6)):
        for g in range(SETS):
            east = west = jnp.zeros((GROUP, LANES), F32)
            for i in range(min(6, rows - 6 * block)):
                value = found[6 * block + i - (SUBSTEPS - 1), g]
                here = (place >= 3 * i) & (place < 3 * i + 3)
                east = jnp.where(here, shift(value, 3 * i - 3), east)
                west = jnp.where(here, shift(value, 3 * i - HALF), west)
            at = pl.ds((block * SETS + g) * GROUP, GROUP)
            east_ref[at, :] = east
            west_ref[at, :] = west


def coupling(m, s, m_n, s_n):
    return 0.5 * (s + s_n) * m * m_n


def factors(wet, spread, rows):
    north = {
        row: coupling(wet[row], spread[row], wet[row + 1], spread[row + 1])
        for row in range(rows[0] - 1, rows[-1] + 1)
    }
    found = {}
    for row in rows:
        m, s = wet[row], spread[row]
        east = coupling(m, s, shift(m, -1), shift(s, -1))
        west = shift(east, 1)
        south = north[row - 1]
        found[row] = (1.0 - (north[row] + south + east + west), north[row], south, east, west)
    return found


def substep(value, row, weight):
    centre = value[row]
    return (
        weight[0] * centre
        + (weight[1] * value[row + 1] + weight[2] * value[row - 1])
        + (weight[3] * shift(centre, -1) + weight[4] * shift(centre, 1))
    )


def tile_kernel(height, chunks, x_ref, mask_ref, diff_ref, a_ref, b_ref, out_ref, coef):
    odd = jnp.full((GROUP, LANES), is_odd()) == 1
    stride = (chunks + 1) * GROUP
    low, high = -(SUBSTEPS - 1), height + SUBSTEPS - 1

    def wide(ref, row):
        return jnp.broadcast_to(ref[row : row + 1, :].astype(F32), (GROUP, LANES))

    wet, spread = {}, {}
    for row in range(height):
        wet[row] = wide(mask_ref, row)
        spread[row] = wide(diff_ref, row)
    for d in range(SUBSTEPS):
        at = d * stride + chunks * GROUP
        for held, row in ((wet, at), (spread, at + 1)):
            first, second = wide(a_ref, row), wide(b_ref, row)
            held[height + d] = jnp.where(odd, first, second)
            held[-1 - d] = jnp.where(odd, second, first)
    weights = factors(wet, spread, range(low, high))
    for row in range(low, high):
        for i in range(5):
            coef[row - low, i] = weights[row][i]

    def one(c):
        rows = pl.ds(c * GROUP, GROUP)
        value = {row: x_ref[row, rows, :] for row in range(height)}
        for d in range(SUBSTEPS):
            value[height + d], value[-1 - d] = pick_rows(
                odd, a_ref, b_ref, pl.ds(d * stride + c * GROUP, GROUP)
            )
        for s in range(SUBSTEPS):
            reach = SUBSTEPS - 1 - s
            value = {
                row: substep(value, row, [coef[row - low, i] for i in range(5)])
                for row in range(-reach, height + reach)
            }
        for row in range(height):
            out_ref[row, rows, :] = value[row]

    def pair(i, unused):
        one(2 * i)
        one(2 * i + 1)
        return unused

    lax.fori_loop(0, chunks // 2, pair, 0)


def edge_kernel(
    height, chunks, parts, y_ref, a_ref, b_ref, p_ref, fe_ref, fw_ref, out_ref, final, tile, sems
):
    lane = lane_iota()
    place = lane % STRIP
    strips = own_strips(height, chunks, a_ref, b_ref, p_ref, SUBSTEPS)
    low = -(SUBSTEPS - 1)
    for (row, g), own in strips.items():
        value = jnp.where(place >= 2 * HALF, shift(own, HALF), own)
        at = row - low
        if 0 <= at < height + 2 * (SUBSTEPS - 1):
            block, i = at // 6, at % 6
            rows = pl.ds((block * SETS + g) * GROUP, GROUP)
            east = shift(fe_ref[rows, :], HALF - 3 * i)
            west = shift(fw_ref[rows, :], HALF + 3 - 3 * i)
            value = jnp.where(
                (place >= HALF) & (place < 2 * HALF), jnp.where(place < 9, east, west), value
            )
        strips[row, g] = value
    which, base = base_of(chunks)
    wet, spread = {}, {}
    for row in range(-SUBSTEPS, height + SUBSTEPS):
        value = strips[row, which]
        for held, i in ((wet, 0), (spread, 1)):
            held[row] = take_lanes(
                jnp.broadcast_to(value[i : i + 1, :], (GROUP, LANES)), base + place
            )
    weights = factors(wet, spread, range(low, height - low))
    for g in range(SETS):
        value = {row: strips[row, g] for row in range(-SUBSTEPS, height + SUBSTEPS)}
        for s in range(SUBSTEPS):
            reach = SUBSTEPS - 1 - s
            value = {
                row: substep(value, row, weights[row]) for row in range(-reach, height + reach)
            }
        for row in range(height):
            final[row, g] = jnp.where(
                (place >= HALF) & (place < HALF + 3), shift(value[row], -HALF), value[row]
            )
    at_edge = (lane < 3) | (lane >= LANES - 3)
    each = chunks // parts
    size = each * GROUP * height
    copies = []
    for p in range(parts):
        for c in range(p * each, (p + 1) * each):
            which, base = base_of(c)
            for row in range(height):
                pulled = shift(final[row, which], LANES - 3 - (base + 3))
                tile[pl.ds(c * GROUP * height + row, GROUP, stride=height), :] = jnp.where(
                    at_edge, pulled, y_ref[row, pl.ds(c * GROUP, GROUP), :]
                )
        copy = pltpu.make_async_copy(
            tile.at[pl.ds(p * size, size)], out_ref.at[pl.ds(p * size, size)], sems.at[p]
        )
        copy.start()
        copies.append(copy)
    for copy in copies:
        copy.wait()


def remap_kernel(
    tracers,
    levels,
    height,
    owners,
    owner_ref,
    x_ref,
    cell_ref,
    column_ref,
    weight_ref,
    out_ref,
    even_ref,
    odd_ref,
    total_ref,
    owners_ref,
    sem,
):
    copy = pltpu.make_async_copy(owner_ref, owners_ref, sem)
    copy.start()
    pad = 2 * GROUP
    groups = cell_ref.shape[0] // GROUP
    total_ref[...] = jnp.zeros_like(total_ref)
    column = lax.broadcasted_iota(jnp.int32, (ACOL, LANES), 0)

    def gather(g, picked_ref):
        rows = pl.ds(g * GROUP, GROUP)
        cell = cell_ref[rows, :]
        at_lane = cell % LANES
        at_row = cell // LANES
        found = [jnp.zeros((GROUP, LANES), F32)] * tracers
        for row in range(height):
            here = at_row == row
            for k in range(tracers):
                source = jnp.broadcast_to(x_ref[row, k * levels : k * levels + 1, :], (GROUP, LANES))
                found[k] = jnp.where(here, take_lanes(source, at_lane), found[k])
        weight = weight_ref[rows, :]
        for k in range(tracers):
            picked_ref[pl.ds(k, GROUP, stride=pad), :] = found[k] * weight

    def add(g, picked_ref):
        for j in range(GROUP):
            block = g * GROUP + j
            value = picked_ref[pl.ds(j * pad, pad), :]
            coarse = value.astype(jnp.bfloat16)
            fine = (value - coarse.astype(F32)).astype(jnp.bfloat16)
            chosen = (column == column_ref[pl.ds(block, 1), :]).astype(F32).astype(jnp.bfloat16)
            product = lax.dot_general(
                jnp.concatenate([coarse, fine], axis=0),
                chosen,
                (((1,), (1,)), ((), ())),
                preferred_element_type=F32,
            )
            owner = owners_ref[block]
            total_ref[owner] = total_ref[owner] + (product[:pad] + product[pad:])

    def two(i, unused):
        gather(2 * i + 1, odd_ref)
        add(2 * i, even_ref)
        gather(2 * i + 2, even_ref)
        add(2 * i + 1, odd_ref)
        return unused

    gather(0, even_ref)
    copy.wait()
    lax.fori_loop(0, groups // 2 - 1, two, 0)
    gather(groups - 1, odd_ref)
    add(groups - 2, even_ref)
    add(groups - 1, odd_ref)

    def write(o, unused):
        for half in range(ACOL // LANES):
            out_ref[o, pl.ds(half * tracers, tracers), :] = total_ref[
                o, pl.ds(0, tracers), pl.ds(half * LANES, LANES)
            ]
        return unused

    lax.fori_loop(0, owners, write, 0)


def sum_kernel(tracers, parts_ref, out_ref):
    total = jnp.sum(parts_ref[...], axis=0)
    for half in range(ACOL // LANES):
        out_ref[:, half * LANES : (half + 1) * LANES] = total[half * tracers : (half + 1) * tracers]


def routes(lon, lat):
    def device(i, j):
        return i * lat + j

    def swaps(first, stop):
        found = []
        for i in range(lon):
            for j in range(first, stop, 2):
                found += [(device(i, j), device(i, j + 1)), (device(i, j + 1), device(i, j))]
        return found

    fold = [(device(i, lat - 1), device(lon - 1 - i, lat - 1)) for i in range(lon)]
    east = [(device(i, j), device((i + 1) % lon, j)) for i in range(lon) for j in range(lat)]
    west = [(b, a) for a, b in east]
    return swaps(1, lat - 1) + fold, swaps(0, lat), east, west


def in_vmem(array):
    return pltpu.with_memory_space_constraint(array, pltpu.VMEM)


def in_hbm(array):
    return pltpu.with_memory_space_constraint(array, pltpu.HBM)


def vmem():
    return pl.BlockSpec(memory_space=pltpu.VMEM)


def anywhere():
    return pl.BlockSpec(memory_space=pltpu.HBM)


def settings(microseconds):
    return dict(
        compiler_params=pltpu.CompilerParams(vmem_limit_bytes=16 * 1024 * 1024),
        cost_estimate=pl.CostEstimate(
            flops=0, transcendentals=0, bytes_accessed=int(microseconds * 3.5e6)
        ),
    )


def parts_of(chunks):
    return 5 if chunks % 5 == 0 else 1


def pack(height, layers, flat, ocean_mask, diffusivity):
    chunks = layers // GROUP
    parts = parts_of(chunks)
    with jax.named_scope("pack"):
        return pl.pallas_call(
            functools.partial(pack_kernel, height, chunks, parts),
            **settings(2),
            out_shape=(
                pltpu.VMEM((message_rows(layers)[1], LANES), F32),
                pltpu.VMEM((message_rows(layers)[1], LANES), F32),
                pltpu.VMEM((height, SETS, GROUP, LANES), F32),
                pltpu.VMEM((height, layers, LANES), F32),
            ),
            in_specs=[anywhere()] * 3,
            out_specs=(vmem(),) * 4,
            scratch_shapes=[
                pltpu.VMEM(flat.shape, F32),
                pltpu.VMEM(ocean_mask.shape, ocean_mask.dtype),
                pltpu.VMEM(diffusivity.shape, F32),
                pltpu.SemaphoreType.DMA((parts + 2,)),
            ],
        )(in_hbm(flat), in_hbm(ocean_mask), in_hbm(diffusivity))


def remap(owners, tracers, levels, x, remap_cell, remap_column, remap_weight, remap_owner):
    blocks = remap_cell.shape[0]
    height = x.shape[0]
    with jax.named_scope("remap"):
        return pl.pallas_call(
            functools.partial(remap_kernel, tracers, levels, height, owners),
            **settings(6),
            out_shape=pltpu.VMEM((owners, 3 * GROUP, LANES), F32),
            in_specs=[anywhere()] + [vmem()] * 4,
            out_specs=vmem(),
            scratch_shapes=[
                pltpu.VMEM((2 * GROUP * GROUP, LANES), F32),
                pltpu.VMEM((2 * GROUP * GROUP, LANES), F32),
                pltpu.VMEM((owners, 2 * GROUP, ACOL), F32),
                pltpu.SMEM((blocks,), jnp.int32),
                pltpu.SemaphoreType.DMA,
            ],
        )(
            in_hbm(remap_owner.reshape(-1)),
            in_vmem(x),
            in_vmem(remap_cell),
            in_vmem(remap_column),
            in_vmem(remap_weight),
        )


def columns(height, layers, got_a, got_b, p):
    rows = -(-(height + 2 * (SUBSTEPS - 1)) // 6) * SETS * GROUP
    with jax.named_scope("columns"):
        return pl.pallas_call(
            functools.partial(columns_kernel, height, layers // GROUP),
            **settings(1),
            out_shape=(pltpu.VMEM((rows, LANES), F32), pltpu.VMEM((rows, LANES), F32)),
            in_specs=[vmem()] * 3,
            out_specs=(vmem(), vmem()),
        )(in_vmem(got_a), in_vmem(got_b), in_vmem(p))


def tile_steps(height, layers, x, ocean_mask, diffusivity, got_a, got_b):
    with jax.named_scope("tile"):
        return pl.pallas_call(
            functools.partial(tile_kernel, height, layers // GROUP),
            **settings(4),
            out_shape=pltpu.VMEM(x.shape, F32),
            in_specs=[vmem()] * 5,
            out_specs=vmem(),
            scratch_shapes=[pltpu.VMEM((height + 2 * (SUBSTEPS - 1), 5, GROUP, LANES), F32)],
        )(in_vmem(x), in_vmem(ocean_mask), in_vmem(diffusivity), in_vmem(got_a), in_vmem(got_b))


def edge_steps(height, layers, y, got_a, got_b, p, from_east, from_west):
    chunks = layers // GROUP
    parts = parts_of(chunks)
    with jax.named_scope("edges"):
        return pl.pallas_call(
            functools.partial(edge_kernel, height, chunks, parts),
            **settings(4),
            out_shape=jax.ShapeDtypeStruct((layers * height, LANES), F32),
            in_specs=[vmem()] * 6,
            out_specs=anywhere(),
            scratch_shapes=[
                pltpu.VMEM((height, SETS, GROUP, LANES), F32),
                pltpu.VMEM((layers * height, LANES), F32),
                pltpu.SemaphoreType.DMA((parts,)),
            ],
        )(
            in_vmem(y),
            in_vmem(got_a),
            in_vmem(got_b),
            in_vmem(p),
            in_vmem(from_east),
            in_vmem(from_west),
        )


def on_device(lon, lat, tracer, ocean_mask, diffusivity, remap_cell, remap_column, remap_weight, remap_owner):
    tracers, levels, height, breadth = tracer.shape
    layers = tracers * levels
    both = ("lon", "lat")
    route_a, route_b, route_east, route_west = routes(lon, lat)
    flat = tracer.reshape(layers * height, breadth)

    send_a, send_b, p, x = pack(height, layers, flat, ocean_mask, diffusivity)
    got_a = lax.ppermute(send_a, both, route_a)
    got_b = lax.ppermute(send_b, both, route_b)

    partial = remap(
        lon * lat, tracers, levels, x, remap_cell, remap_column, remap_weight, remap_owner
    )
    parts = lax.all_to_all(partial, both, 0, 0, tiled=True)

    send_east, send_west = columns(height, layers, got_a, got_b, p)
    from_west = lax.ppermute(send_east, both, route_east)
    from_east = lax.ppermute(send_west, both, route_west)

    y = tile_steps(height, layers, x, ocean_mask, diffusivity, got_a, got_b)
    updated = edge_steps(height, layers, y, got_a, got_b, p, from_east, from_west)

    with jax.named_scope("sum"):
        atmosphere = pl.pallas_call(
            functools.partial(sum_kernel, tracers),
            **settings(1),
            out_shape=jax.ShapeDtypeStruct((tracers, ACOL), F32),
            in_specs=[vmem()],
            out_specs=vmem(),
        )(in_vmem(parts))
    return updated.reshape(tracer.shape), atmosphere


def solution(mesh):
    in_specs = (
        P("member", None, "lat", "lon"),
        P("lat", "lon"),
        P("lat", "lon"),
        P(("lon", "lat"), None),
        P(("lon", "lat"), None),
        P(("lon", "lat"), None),
        P(("lon", "lat"), None),
    )
    out_specs = (P("member", None, "lat", "lon"), P("member", ("lon", "lat")))
    return jax.shard_map(
        functools.partial(on_device, mesh.shape["lon"], mesh.shape["lat"]),
        mesh=mesh,
        in_specs=in_specs,
        out_specs=out_specs,
        check_vma=False,
    )
```

```python
import functools

import jax
import jax.numpy as jnp
from jax import lax
from jax.experimental import pallas as pl
from jax.experimental.pallas import tpu as pltpu
from jax.sharding import PartitionSpec as P

ACOL = 256
SUBSTEPS = 3
LANES = 128
GROUP = 8
F32 = jnp.float32

STRIP = 18
PER = 7
SETS = 3
HALF = 6
SLOTS = 5


def lane_iota():
    return lax.broadcasted_iota(jnp.int32, (GROUP, LANES), 1)


def shift(value, amount):
    amount = amount % LANES
    return pltpu.roll(value, amount, 1) if amount else value


def take_lanes(value, index):
    return jnp.take_along_axis(value, index, axis=1)


def is_odd():
    return lax.axis_index("lat") % 2


def register(row, which):
    return pl.ds((row * SETS + which) * GROUP, GROUP)


def base_of(chunk):
    return chunk // PER, STRIP * (chunk % PER)


def message_rows(layers):
    return SUBSTEPS * (layers + GROUP), SUBSTEPS * (layers + GROUP) + SUBSTEPS * SETS * GROUP


def pack_kernel(
    height,
    chunks,
    parts,
    levels,
    tracer_ref,
    mask_ref,
    diff_ref,
    a_ref,
    b_ref,
    p_ref,
    surface_ref,
    tile,
    wet_tile,
    spread_tile,
    sems,
):
    odd = jnp.full((GROUP, LANES), is_odd()) == 1
    top = (lax.axis_index("lat") == lax.axis_size("lat") - 1).astype(jnp.int32)
    each = chunks // parts
    size = each * GROUP * height
    copies = [
        pltpu.make_async_copy(
            tracer_ref.at[pl.ds(p * size, size)], tile.at[pl.ds(p * size, size)], sems.at[p]
        )
        for p in range(parts)
    ]
    copies.append(pltpu.make_async_copy(mask_ref, wet_tile, sems.at[parts]))
    copies.append(pltpu.make_async_copy(diff_ref, spread_tile, sems.at[parts + 1]))
    for copy in copies:
        copy.start()

    lane = lane_iota()
    place = lane % STRIP
    is_top = jnp.full((GROUP, LANES), top) == 1
    flip = jnp.where(is_top, LANES - 1 - lane, lane)
    flip_strip = jnp.where(is_top & (place < 2 * HALF), lane - place + 2 * HALF - 1 - place, lane)
    stride = (chunks + 1) * GROUP
    strips_at = SUBSTEPS * stride

    def send(c, value):
        for d in range(SUBSTEPS):
            rows = pl.ds(d * stride + c * GROUP, GROUP)
            near, far = value[d], value[height - 1 - d]
            a_ref[rows, :] = take_lanes(jnp.where(odd, far, near), flip)
            b_ref[rows, :] = jnp.where(odd, near, far)

    strips = {}

    def edge(c, value):
        which, base = base_of(c)
        here = (lane >= base) & (lane < base + 2 * HALF)
        for row in range(height):
            before = strips.get((row, which), jnp.zeros((GROUP, LANES), F32))
            strips[row, which] = jnp.where(here, shift(value[row], base + HALF), before)

    for p in range(parts):
        copies[p].wait()
        for c in range(p * each, (p + 1) * each):
            value = {}
            for row in range(height):
                value[row] = tile[pl.ds(c * GROUP * height + row, GROUP, stride=height), :]
            send(c, value)
            edge(c, value)

    for k in range(chunks * GROUP // levels):
        surface_ref[k] = tile[pl.ds(k * levels * height, height), :]
    copies[parts].wait()
    copies[parts + 1].wait()
    sub = lax.broadcasted_iota(jnp.int32, (GROUP, LANES), 0)
    value = {}
    for row in range(height):
        wet = jnp.broadcast_to(wet_tile[row : row + 1, :].astype(F32), (GROUP, LANES))
        spread = jnp.broadcast_to(spread_tile[row : row + 1, :], (GROUP, LANES))
        value[row] = jnp.where(sub == 0, wet, jnp.where(sub == 1, spread, 0.0))
    send(chunks, value)
    edge(chunks, value)

    zero = jnp.zeros((GROUP, LANES), F32)
    for row in range(height):
        for g in range(SETS):
            p_ref[register(row, g), :] = strips.get((row, g), zero)
    for d in range(SUBSTEPS):
        for g in range(SETS):
            near, far = strips.get((d, g), zero), strips.get((height - 1 - d, g), zero)
            rows = pl.ds(strips_at + (d * SETS + g) * GROUP, GROUP)
            a_ref[rows, :] = take_lanes(jnp.where(odd, far, near), flip_strip)
            b_ref[rows, :] = jnp.where(odd, near, far)


def pick_rows(odd, a_ref, b_ref, rows):
    first = a_ref[rows, :]
    second = b_ref[rows, :]
    return jnp.where(odd, first, second), jnp.where(odd, second, first)


def own_strips(height, chunks, a_ref, b_ref, p_ref, depth):
    odd = jnp.full((GROUP, LANES), is_odd()) == 1
    strips_at = SUBSTEPS * (chunks + 1) * GROUP
    found = {}
    for g in range(SETS):
        for row in range(height):
            found[row, g] = p_ref[register(row, g), :]
        for d in range(depth):
            rows = pl.ds(strips_at + (d * SETS + g) * GROUP, GROUP)
            found[height + d, g], found[-1 - d, g] = pick_rows(odd, a_ref, b_ref, rows)
    return found


def columns_kernel(height, chunks, a_ref, b_ref, p_ref, east_ref, west_ref):
    found = own_strips(height, chunks, a_ref, b_ref, p_ref, SUBSTEPS - 1)
    place = lane_iota() % STRIP
    rows = height + 2 * (SUBSTEPS - 1)
    for block in range(-(-rows // SLOTS)):
        for g in range(SETS):
            east = west = jnp.zeros((GROUP, LANES), F32)
            for i in range(min(SLOTS, rows - SLOTS * block)):
                value = found[SLOTS * block + i - (SUBSTEPS - 1), g]
                here = (place >= 3 * i) & (place < 3 * i + 3)
                after = (place >= 3 * i + 3) & (place < 3 * i + 6)
                east = jnp.where(after, shift(value, 3 * i), east)
                west = jnp.where(here, shift(value, 3 * i - HALF), west)
            at = pl.ds((block * SETS + g) * GROUP, GROUP)
            east_ref[at, :] = east
            west_ref[at, :] = west


def coupling(m, s, m_n, s_n):
    return 0.5 * (s + s_n) * m * m_n


def factors(wet, spread, rows):
    north = {
        row: coupling(wet[row], spread[row], wet[row + 1], spread[row + 1])
        for row in range(rows[0] - 1, rows[-1] + 1)
    }
    found = {}
    for row in rows:
        m, s = wet[row], spread[row]
        east = coupling(m, s, shift(m, -1), shift(s, -1))
        west = shift(east, 1)
        south = north[row - 1]
        found[row] = (1.0 - (north[row] + south + east + west), north[row], south, east, west)
    return found


def substep(value, row, weight):
    centre = value[row]
    return (
        weight[0] * centre
        + (weight[1] * value[row + 1] + weight[2] * value[row - 1])
        + (weight[3] * shift(centre, -1) + weight[4] * shift(centre, 1))
    )


def tile_kernel(
    height,
    chunks,
    parts,
    tracer_ref,
    mask_ref,
    diff_ref,
    a_ref,
    b_ref,
    p_ref,
    out_ref,
    strips_ref,
    coef,
    tile,
    sems,
):
    each = chunks // parts
    size = each * GROUP * height
    copies = [
        pltpu.make_async_copy(
            tracer_ref.at[pl.ds(p * size, size)], tile.at[pl.ds(p * size, size)], sems.at[p]
        )
        for p in range(parts)
    ]
    for copy in copies:
        copy.start()
    odd = jnp.full((GROUP, LANES), is_odd()) == 1
    stride = (chunks + 1) * GROUP
    low, high = -(SUBSTEPS - 1), height + SUBSTEPS - 1

    def wide(ref, row):
        return jnp.broadcast_to(ref[row : row + 1, :].astype(F32), (GROUP, LANES))

    wet, spread = {}, {}
    for row in range(height):
        wet[row] = wide(mask_ref, row)
        spread[row] = wide(diff_ref, row)
    for d in range(SUBSTEPS):
        at = d * stride + chunks * GROUP
        for held, row in ((wet, at), (spread, at + 1)):
            first, second = wide(a_ref, row), wide(b_ref, row)
            held[height + d] = jnp.where(odd, first, second)
            held[-1 - d] = jnp.where(odd, second, first)
    weights = factors(wet, spread, range(low, high))
    for row in range(low, high):
        for i in range(5):
            coef[row - low, i] = weights[row][i]

    def one(c):
        rows = pl.ds(c * GROUP, GROUP)
        value = {
            row: tile[pl.ds(c * (GROUP * height) + row, GROUP, stride=height), :]
            for row in range(height)
        }
        for d in range(SUBSTEPS):
            value[height + d], value[-1 - d] = pick_rows(
                odd, a_ref, b_ref, pl.ds(d * stride + c * GROUP, GROUP)
            )
        for s in range(SUBSTEPS):
            reach = SUBSTEPS - 1 - s
            value = {
                row: substep(value, row, [coef[row - low, i] for i in range(5)])
                for row in range(-reach, height + reach)
            }
        for row in range(height):
            out_ref[row, rows, :] = value[row]

    def pair(i, unused):
        one(2 * i)
        one(2 * i + 1)
        return unused

    place = lane_iota() % STRIP
    for (row, g), own in own_strips(height, chunks, a_ref, b_ref, p_ref, SUBSTEPS).items():
        strips_ref[register(row + SUBSTEPS, g), :] = jnp.where(
            place >= 2 * HALF, shift(own, HALF), own
        )
    for p in range(parts):
        copies[p].wait()
        lax.fori_loop(p * each // 2, (p + 1) * each // 2, pair, 0)


def edge_kernel(
    height,
    chunks,
    parts,
    tracers,
    y_ref,
    strips_ref,
    fe_ref,
    fw_ref,
    parts_ref,
    out_ref,
    atmosphere_ref,
    strip,
    coef,
    final,
    tile,
    sums,
    sems,
):
    lane = lane_iota()
    place = lane % STRIP
    low, high = -(SUBSTEPS - 1), height + SUBSTEPS - 1

    def with_halo(row, g):
        own = strips_ref[register(row + SUBSTEPS, g), :]
        if not low <= row < high:
            return own
        block, i = (row - low) // SLOTS, (row - low) % SLOTS
        rows = pl.ds((block * SETS + g) * GROUP, GROUP)
        both = shift(jnp.where(place < 3 * i + 3, fe_ref[rows, :], fw_ref[rows, :]), HALF - 3 * i)
        return jnp.where((place >= HALF) & (place < 2 * HALF), both, own)

    which, base = base_of(chunks)
    wet, spread = {}, {}
    for row in range(-SUBSTEPS, height + SUBSTEPS):
        value = with_halo(row, which)
        strip[row + SUBSTEPS, which] = value
        for held, i in ((wet, 0), (spread, 1)):
            held[row] = take_lanes(
                jnp.broadcast_to(value[i : i + 1, :], (GROUP, LANES)), base + place
            )
    weights = factors(wet, spread, range(low, high))
    for row in range(low, high):
        for i in range(5):
            coef[row - low, i] = weights[row][i]
    for g in range(SETS):
        value = {}
        for row in range(-SUBSTEPS, height + SUBSTEPS):
            value[row] = strip[row + SUBSTEPS, g] if g == which else with_halo(row, g)
        for s in range(SUBSTEPS):
            reach = SUBSTEPS - 1 - s
            value = {
                row: substep(value, row, [coef[row - low, i] for i in range(5)])
                for row in range(-reach, height + reach)
            }
        for row in range(height):
            final[row, g] = jnp.where(
                (place >= HALF) & (place < HALF + 3), shift(value[row], -HALF), value[row]
            )
    at_edge = (lane < 3) | (lane >= LANES - 3)
    each = chunks // parts
    size = each * GROUP * height
    copies = []
    for p in range(parts):
        for c in range(p * each, (p + 1) * each):
            which, base = base_of(c)
            for row in range(height):
                pulled = shift(final[row, which], LANES - 3 - (base + 3))
                tile[pl.ds(c * GROUP * height + row, GROUP, stride=height), :] = jnp.where(
                    at_edge, pulled, y_ref[row, pl.ds(c * GROUP, GROUP), :]
                )
        copy = pltpu.make_async_copy(
            tile.at[pl.ds(p * size, size)], out_ref.at[pl.ds(p * size, size)], sems.at[p]
        )
        copy.start()
        copies.append(copy)
    total = jnp.sum(parts_ref[...], axis=0)
    for half in range(ACOL // LANES):
        sums[:, half * LANES : (half + 1) * LANES] = total[half * tracers : (half + 1) * tracers]
    copy = pltpu.make_async_copy(sums, atmosphere_ref, sems.at[parts])
    copy.start()
    copies.append(copy)
    for copy in copies:
        copy.wait()


def remap_kernel(
    tracers,
    height,
    owners,
    owner_ref,
    surface_ref,
    cell_ref,
    column_ref,
    weight_ref,
    out_ref,
    even_ref,
    odd_ref,
    total_ref,
    owners_ref,
    sem,
):
    copy = pltpu.make_async_copy(owner_ref, owners_ref, sem)
    copy.start()
    pad = 2 * GROUP
    groups = cell_ref.shape[0] // GROUP
    total_ref[...] = jnp.zeros_like(total_ref)
    column = lax.broadcasted_iota(jnp.int32, (ACOL, LANES), 0)

    def gather(g, picked_ref):
        rows = pl.ds(g * GROUP, GROUP)
        cell = cell_ref[rows, :]
        at_lane = cell % LANES
        at_row = cell // LANES
        found = [jnp.zeros((GROUP, LANES), F32)] * tracers
        for row in range(height):
            here = at_row == row
            for k in range(tracers):
                source = jnp.broadcast_to(surface_ref[k, row : row + 1, :], (GROUP, LANES))
                found[k] = jnp.where(here, take_lanes(source, at_lane), found[k])
        weight = weight_ref[rows, :]
        for k in range(tracers):
            picked_ref[pl.ds(k, GROUP, stride=pad), :] = found[k] * weight

    def add(g, picked_ref):
        for j in range(GROUP):
            block = g * GROUP + j
            value = picked_ref[pl.ds(j * pad, pad), :]
            coarse = value.astype(jnp.bfloat16)
            fine = (value - coarse.astype(F32)).astype(jnp.bfloat16)
            chosen = (column == column_ref[pl.ds(block, 1), :]).astype(F32).astype(jnp.bfloat16)
            product = lax.dot_general(
                jnp.concatenate([coarse, fine], axis=0),
                chosen,
                (((1,), (1,)), ((), ())),
                preferred_element_type=F32,
            )
            owner = owners_ref[block]
            total_ref[owner] = total_ref[owner] + (product[:pad] + product[pad:])

    def two(i, unused):
        gather(2 * i + 1, odd_ref)
        add(2 * i, even_ref)
        gather(2 * i + 2, even_ref)
        add(2 * i + 1, odd_ref)
        return unused

    gather(0, even_ref)
    copy.wait()
    lax.fori_loop(0, groups // 2 - 1, two, 0)
    gather(groups - 1, odd_ref)
    add(groups - 2, even_ref)
    add(groups - 1, odd_ref)

    def write(o, unused):
        for half in range(ACOL // LANES):
            out_ref[o, pl.ds(half * tracers, tracers), :] = total_ref[
                o, pl.ds(0, tracers), pl.ds(half * LANES, LANES)
            ]
        return unused

    lax.fori_loop(0, owners, write, 0)


def routes(lon, lat):
    def device(i, j):
        return i * lat + j

    def swaps(first, stop):
        found = []
        for i in range(lon):
            for j in range(first, stop, 2):
                found += [(device(i, j), device(i, j + 1)), (device(i, j + 1), device(i, j))]
        return found

    fold = [(device(i, lat - 1), device(lon - 1 - i, lat - 1)) for i in range(lon)]
    east = [(device(i, j), device((i + 1) % lon, j)) for i in range(lon) for j in range(lat)]
    west = [(b, a) for a, b in east]
    return swaps(1, lat - 1) + fold, swaps(0, lat), east, west


def in_vmem(array):
    return pltpu.with_memory_space_constraint(array, pltpu.VMEM)


def in_hbm(array):
    return pltpu.with_memory_space_constraint(array, pltpu.HBM)


def vmem():
    return pl.BlockSpec(memory_space=pltpu.VMEM)


def anywhere():
    return pl.BlockSpec(memory_space=pltpu.HBM)


def settings(microseconds):
    return dict(
        compiler_params=pltpu.CompilerParams(vmem_limit_bytes=16 * 1024 * 1024),
        cost_estimate=pl.CostEstimate(
            flops=0, transcendentals=0, bytes_accessed=int(microseconds * 3.5e6)
        ),
    )


def parts_of(chunks):
    return 5 if chunks % 5 == 0 else 1


def pack(height, layers, levels, flat, ocean_mask, diffusivity):
    chunks = layers // GROUP
    parts = parts_of(chunks)
    with jax.named_scope("pack"):
        return pl.pallas_call(
            functools.partial(pack_kernel, height, chunks, parts, levels),
            **settings(2),
            out_shape=(
                pltpu.VMEM((message_rows(layers)[1], LANES), F32),
                pltpu.VMEM((message_rows(layers)[1], LANES), F32),
                pltpu.VMEM((height * SETS * GROUP, LANES), F32),
                pltpu.VMEM((layers // levels, height, LANES), F32),
            ),
            in_specs=[anywhere()] * 3,
            out_specs=(vmem(),) * 4,
            scratch_shapes=[
                pltpu.VMEM(flat.shape, F32),
                pltpu.VMEM(ocean_mask.shape, ocean_mask.dtype),
                pltpu.VMEM(diffusivity.shape, F32),
                pltpu.SemaphoreType.DMA((parts + 2,)),
            ],
        )(in_hbm(flat), in_hbm(ocean_mask), in_hbm(diffusivity))


def remap(owners, surface, remap_cell, remap_column, remap_weight, remap_owner):
    blocks = remap_cell.shape[0]
    tracers, height, unused = surface.shape
    with jax.named_scope("remap"):
        return pl.pallas_call(
            functools.partial(remap_kernel, tracers, height, owners),
            **settings(6),
            out_shape=pltpu.VMEM((owners, 3 * GROUP, LANES), F32),
            in_specs=[anywhere()] + [vmem()] * 4,
            out_specs=vmem(),
            scratch_shapes=[
                pltpu.VMEM((2 * GROUP * GROUP, LANES), F32),
                pltpu.VMEM((2 * GROUP * GROUP, LANES), F32),
                pltpu.VMEM((owners, 2 * GROUP, ACOL), F32),
                pltpu.SMEM((blocks,), jnp.int32),
                pltpu.SemaphoreType.DMA,
            ],
        )(
            in_hbm(remap_owner.reshape(-1)),
            in_vmem(surface),
            in_vmem(remap_cell),
            in_vmem(remap_column),
            in_vmem(remap_weight),
        )


def columns(height, layers, got_a, got_b, p):
    rows = -(-(height + 2 * (SUBSTEPS - 1)) // SLOTS) * SETS * GROUP
    with jax.named_scope("columns"):
        return pl.pallas_call(
            functools.partial(columns_kernel, height, layers // GROUP),
            **settings(1),
            out_shape=(pltpu.VMEM((rows, LANES), F32), pltpu.VMEM((rows, LANES), F32)),
            in_specs=[vmem()] * 3,
            out_specs=(vmem(), vmem()),
        )(in_vmem(got_a), in_vmem(got_b), in_vmem(p))


def tile_steps(height, layers, flat, ocean_mask, diffusivity, got_a, got_b, p):
    chunks = layers // GROUP
    parts = parts_of(chunks)
    with jax.named_scope("tile"):
        return pl.pallas_call(
            functools.partial(tile_kernel, height, chunks, parts),
            **settings(4),
            out_shape=(
                pltpu.VMEM((height, layers, LANES), F32),
                pltpu.VMEM(((height + 2 * SUBSTEPS) * SETS * GROUP, LANES), F32),
            ),
            in_specs=[anywhere()] + [vmem()] * 5,
            out_specs=(vmem(), vmem()),
            scratch_shapes=[
                pltpu.VMEM((height + 2 * (SUBSTEPS - 1), 5, GROUP, LANES), F32),
                pltpu.VMEM(flat.shape, F32),
                pltpu.SemaphoreType.DMA((parts,)),
            ],
        )(
            in_hbm(flat),
            in_vmem(ocean_mask),
            in_vmem(diffusivity),
            in_vmem(got_a),
            in_vmem(got_b),
            in_vmem(p),
        )


def edge_steps(height, layers, tracers, y, strips, from_east, from_west, sums):
    chunks = layers // GROUP
    parts = parts_of(chunks)
    with jax.named_scope("edges"):
        return pl.pallas_call(
            functools.partial(edge_kernel, height, chunks, parts, tracers),
            **settings(3),
            out_shape=(
                jax.ShapeDtypeStruct((layers * height, LANES), F32),
                jax.ShapeDtypeStruct((tracers, ACOL), F32),
            ),
            in_specs=[vmem()] * 5,
            out_specs=(anywhere(), anywhere()),
            scratch_shapes=[
                pltpu.VMEM((height + 2 * SUBSTEPS, SETS, GROUP, LANES), F32),
                pltpu.VMEM((height + 2 * (SUBSTEPS - 1), 5, GROUP, LANES), F32),
                pltpu.VMEM((height, SETS, GROUP, LANES), F32),
                pltpu.VMEM((layers * height, LANES), F32),
                pltpu.VMEM((tracers, ACOL), F32),
                pltpu.SemaphoreType.DMA((parts + 1,)),
            ],
        )(in_vmem(y), in_vmem(strips), in_vmem(from_east), in_vmem(from_west), in_vmem(sums))


def on_device(lon, lat, tracer, ocean_mask, diffusivity, remap_cell, remap_column, remap_weight, remap_owner):
    tracers, levels, height, breadth = tracer.shape
    layers = tracers * levels
    both = ("lon", "lat")
    route_a, route_b, route_east, route_west = routes(lon, lat)
    flat = tracer.reshape(layers * height, breadth)

    send_a, send_b, p, surface = pack(height, layers, levels, flat, ocean_mask, diffusivity)
    got_a = lax.ppermute(send_a, both, route_a)
    got_b = lax.ppermute(send_b, both, route_b)

    partial = remap(lon * lat, surface, remap_cell, remap_column, remap_weight, remap_owner)
    partial, got_a, got_b = lax.optimization_barrier((partial, got_a, got_b))
    parts = lax.all_to_all(partial, both, 0, 0, tiled=True)

    send_east, send_west = columns(height, layers, got_a, got_b, p)
    from_west = lax.ppermute(send_east, both, route_east)
    from_east = lax.ppermute(send_west, both, route_west)

    y, strips = tile_steps(height, layers, flat, ocean_mask, diffusivity, got_a, got_b, p)
    updated, atmosphere = edge_steps(
        height, layers, tracers, y, strips, from_east, from_west, parts
    )
    return updated.reshape(tracer.shape), atmosphere


def solution(mesh):
    in_specs = (
        P("member", None, "lat", "lon"),
        P("lat", "lon"),
        P("lat", "lon"),
        P(("lon", "lat"), None),
        P(("lon", "lat"), None),
        P(("lon", "lat"), None),
        P(("lon", "lat"), None),
    )
    out_specs = (P("member", None, "lat", "lon"), P("member", ("lon", "lat")))
    return jax.shard_map(
        functools.partial(on_device, mesh.shape["lon"], mesh.shape["lat"]),
        mesh=mesh,
        in_specs=in_specs,
        out_specs=out_specs,
        check_vma=False,
    )
```

```python
import functools

import jax
import jax.numpy as jnp
from jax import lax
from jax.experimental import pallas as pl
from jax.experimental.pallas import tpu as pltpu
from jax.sharding import PartitionSpec as P

ACOL = 256
SUBSTEPS = 3
LANES = 128
GROUP = 8
F32 = jnp.float32

STRIP = 18
PER = 7
SETS = 3
HALF = 6
SLOTS = 5


def lane_iota():
    return lax.broadcasted_iota(jnp.int32, (GROUP, LANES), 1)


def shift(value, amount):
    amount = amount % LANES
    return pltpu.roll(value, amount, 1) if amount else value


def take_lanes(value, index):
    return jnp.take_along_axis(value, index, axis=1)


def is_odd():
    return lax.axis_index("lat") % 2


def register(row, which):
    return pl.ds((row * SETS + which) * GROUP, GROUP)


def base_of(chunk):
    return chunk // PER, STRIP * (chunk % PER)


def message_rows(layers):
    return SUBSTEPS * (layers + GROUP), SUBSTEPS * (layers + GROUP) + SUBSTEPS * SETS * GROUP


def pack_kernel(
    height,
    chunks,
    parts,
    levels,
    tracer_ref,
    mask_ref,
    diff_ref,
    owner_ref,
    a_ref,
    b_ref,
    p_ref,
    surface_ref,
    owners_ref,
    tile,
    wet_tile,
    spread_tile,
    sems,
):
    odd = jnp.full((GROUP, LANES), is_odd()) == 1
    top = (lax.axis_index("lat") == lax.axis_size("lat") - 1).astype(jnp.int32)
    each = chunks // parts
    size = each * GROUP * height
    copies = [
        pltpu.make_async_copy(
            tracer_ref.at[pl.ds(p * size, size)], tile.at[pl.ds(p * size, size)], sems.at[p]
        )
        for p in range(parts)
    ]
    copies.append(pltpu.make_async_copy(mask_ref, wet_tile, sems.at[parts]))
    copies.append(pltpu.make_async_copy(diff_ref, spread_tile, sems.at[parts + 1]))
    copies.append(pltpu.make_async_copy(owner_ref, owners_ref, sems.at[parts + 2]))
    for copy in copies:
        copy.start()

    lane = lane_iota()
    place = lane % STRIP
    is_top = jnp.full((GROUP, LANES), top) == 1
    flip = jnp.where(is_top, LANES - 1 - lane, lane)
    flip_strip = jnp.where(is_top & (place < 2 * HALF), lane - place + 2 * HALF - 1 - place, lane)
    stride = (chunks + 1) * GROUP
    strips_at = SUBSTEPS * stride

    def send(c, value):
        for d in range(SUBSTEPS):
            rows = pl.ds(d * stride + c * GROUP, GROUP)
            near, far = value[d], value[height - 1 - d]
            a_ref[rows, :] = take_lanes(jnp.where(odd, far, near), flip)
            b_ref[rows, :] = jnp.where(odd, near, far)

    strips = {}

    def edge(c, value):
        which, base = base_of(c)
        here = (lane >= base) & (lane < base + 2 * HALF)
        for row in range(height):
            before = strips.get((row, which), jnp.zeros((GROUP, LANES), F32))
            strips[row, which] = jnp.where(here, shift(value[row], base + HALF), before)

    for p in range(parts):
        copies[p].wait()
        for c in range(p * each, (p + 1) * each):
            value = {}
            for row in range(height):
                value[row] = tile[pl.ds(c * GROUP * height + row, GROUP, stride=height), :]
            send(c, value)
            edge(c, value)

    for k in range(chunks * GROUP // levels):
        surface_ref[k] = tile[pl.ds(k * levels * height, height), :]
    copies[parts].wait()
    copies[parts + 1].wait()
    copies[parts + 2].wait()
    sub = lax.broadcasted_iota(jnp.int32, (GROUP, LANES), 0)
    value = {}
    for row in range(height):
        wet = jnp.broadcast_to(wet_tile[row : row + 1, :].astype(F32), (GROUP, LANES))
        spread = jnp.broadcast_to(spread_tile[row : row + 1, :], (GROUP, LANES))
        value[row] = jnp.where(sub == 0, wet, jnp.where(sub == 1, spread, 0.0))
    send(chunks, value)
    edge(chunks, value)

    zero = jnp.zeros((GROUP, LANES), F32)
    for row in range(height):
        for g in range(SETS):
            p_ref[register(row, g), :] = strips.get((row, g), zero)
    for d in range(SUBSTEPS):
        for g in range(SETS):
            near, far = strips.get((d, g), zero), strips.get((height - 1 - d, g), zero)
            rows = pl.ds(strips_at + (d * SETS + g) * GROUP, GROUP)
            a_ref[rows, :] = take_lanes(jnp.where(odd, far, near), flip_strip)
            b_ref[rows, :] = jnp.where(odd, near, far)


def beyond_south():
    return jnp.full((GROUP, LANES), lax.axis_index("lat")) == 0


def pick_rows(odd, a_ref, b_ref, rows):
    first = a_ref[rows, :]
    second = b_ref[rows, :]
    return jnp.where(odd, first, second), jnp.where(odd, second, first)


def own_strips(height, chunks, a_ref, b_ref, p_ref, depth):
    odd = jnp.full((GROUP, LANES), is_odd()) == 1
    strips_at = SUBSTEPS * (chunks + 1) * GROUP
    found = {}
    for g in range(SETS):
        for row in range(height):
            found[row, g] = p_ref[register(row, g), :]
        for d in range(depth):
            rows = pl.ds(strips_at + (d * SETS + g) * GROUP, GROUP)
            found[height + d, g], found[-1 - d, g] = pick_rows(odd, a_ref, b_ref, rows)
    return found


def columns_kernel(height, chunks, a_ref, b_ref, p_ref, east_ref, west_ref):
    found = own_strips(height, chunks, a_ref, b_ref, p_ref, SUBSTEPS - 1)
    place = lane_iota() % STRIP
    rows = height + 2 * (SUBSTEPS - 1)
    for block in range(-(-rows // SLOTS)):
        for g in range(SETS):
            east = west = jnp.zeros((GROUP, LANES), F32)
            for i in range(min(SLOTS, rows - SLOTS * block)):
                value = found[SLOTS * block + i - (SUBSTEPS - 1), g]
                here = (place >= 3 * i) & (place < 3 * i + 3)
                after = (place >= 3 * i + 3) & (place < 3 * i + 6)
                east = jnp.where(after, shift(value, 3 * i), east)
                west = jnp.where(here, shift(value, 3 * i - HALF), west)
            at = pl.ds((block * SETS + g) * GROUP, GROUP)
            east_ref[at, :] = east
            west_ref[at, :] = west


def coupling(m, s, m_n, s_n):
    return 0.5 * (s + s_n) * m * m_n


def factors(wet, spread, rows):
    north = {
        row: coupling(wet[row], spread[row], wet[row + 1], spread[row + 1])
        for row in range(rows[0] - 1, rows[-1] + 1)
    }
    found = {}
    for row in rows:
        m, s = wet[row], spread[row]
        east = coupling(m, s, shift(m, -1), shift(s, -1))
        west = shift(east, 1)
        south = north[row - 1]
        found[row] = (1.0 - (north[row] + south + east + west), north[row], south, east, west)
    return found


def substep(value, row, weight):
    centre = value[row]
    return (
        weight[0] * centre
        + (weight[1] * value[row + 1] + weight[2] * value[row - 1])
        + (weight[3] * shift(centre, -1) + weight[4] * shift(centre, 1))
    )


def tile_kernel(
    height,
    chunks,
    parts,
    tracer_ref,
    mask_ref,
    diff_ref,
    a_ref,
    b_ref,
    p_ref,
    out_ref,
    strips_ref,
    coef,
    tile,
    sems,
):
    each = chunks // parts
    size = each * GROUP * height
    copies = [
        pltpu.make_async_copy(
            tracer_ref.at[pl.ds(p * size, size)], tile.at[pl.ds(p * size, size)], sems.at[p]
        )
        for p in range(parts)
    ]
    for copy in copies:
        copy.start()
    odd = jnp.full((GROUP, LANES), is_odd()) == 1
    stride = (chunks + 1) * GROUP
    low, high = -(SUBSTEPS - 1), height + SUBSTEPS - 1

    def wide(ref, row):
        return jnp.broadcast_to(ref[row : row + 1, :].astype(F32), (GROUP, LANES))

    wet, spread = {}, {}
    south = beyond_south()
    for row in range(height):
        wet[row] = wide(mask_ref, row)
        spread[row] = wide(diff_ref, row)
    for d in range(SUBSTEPS):
        at = d * stride + chunks * GROUP
        for held, row in ((wet, at), (spread, at + 1)):
            first, second = wide(a_ref, row), wide(b_ref, row)
            held[height + d] = jnp.where(odd, first, second)
            held[-1 - d] = jnp.where(odd, second, first)
        wet[-1 - d] = jnp.where(south, 0.0, wet[-1 - d])
    weights = factors(wet, spread, range(low, high))
    for row in range(low, high):
        for i in range(5):
            coef[row - low, i] = weights[row][i]

    def one(c):
        rows = pl.ds(c * GROUP, GROUP)
        value = {
            row: tile[pl.ds(c * (GROUP * height) + row, GROUP, stride=height), :]
            for row in range(height)
        }
        for d in range(SUBSTEPS):
            value[height + d], value[-1 - d] = pick_rows(
                odd, a_ref, b_ref, pl.ds(d * stride + c * GROUP, GROUP)
            )
        for s in range(SUBSTEPS):
            reach = SUBSTEPS - 1 - s
            value = {
                row: substep(value, row, [coef[row - low, i] for i in range(5)])
                for row in range(-reach, height + reach)
            }
        for row in range(height):
            out_ref[row, rows, :] = value[row]

    def pair(i, unused):
        one(2 * i)
        one(2 * i + 1)
        return unused

    place = lane_iota() % STRIP
    for (row, g), own in own_strips(height, chunks, a_ref, b_ref, p_ref, SUBSTEPS).items():
        strips_ref[register(row + SUBSTEPS, g), :] = jnp.where(
            place >= 2 * HALF, shift(own, HALF), own
        )
    for p in range(parts):
        copies[p].wait()
        lax.fori_loop(p * each // 2, (p + 1) * each // 2, pair, 0)


def edge_kernel(
    height,
    chunks,
    parts,
    tracers,
    y_ref,
    strips_ref,
    fe_ref,
    fw_ref,
    parts_ref,
    out_ref,
    atmosphere_ref,
    strip,
    coef,
    final,
    tile,
    sums,
    sems,
):
    lane = lane_iota()
    place = lane % STRIP
    low, high = -(SUBSTEPS - 1), height + SUBSTEPS - 1

    def with_halo(row, g):
        own = strips_ref[register(row + SUBSTEPS, g), :]
        if not low <= row < high:
            return own
        block, i = (row - low) // SLOTS, (row - low) % SLOTS
        rows = pl.ds((block * SETS + g) * GROUP, GROUP)
        both = shift(jnp.where(place < 3 * i + 3, fe_ref[rows, :], fw_ref[rows, :]), HALF - 3 * i)
        return jnp.where((place >= HALF) & (place < 2 * HALF), both, own)

    which, base = base_of(chunks)
    wet, spread = {}, {}
    for row in range(-SUBSTEPS, height + SUBSTEPS):
        value = with_halo(row, which)
        strip[row + SUBSTEPS, which] = value
        for held, i in ((wet, 0), (spread, 1)):
            held[row] = take_lanes(
                jnp.broadcast_to(value[i : i + 1, :], (GROUP, LANES)), base + place
            )
        if row < 0:
            wet[row] = jnp.where(beyond_south(), 0.0, wet[row])
    weights = factors(wet, spread, range(low, high))
    for row in range(low, high):
        for i in range(5):
            coef[row - low, i] = weights[row][i]
    for g in range(SETS):
        value = {}
        for row in range(-SUBSTEPS, height + SUBSTEPS):
            value[row] = strip[row + SUBSTEPS, g] if g == which else with_halo(row, g)
        for s in range(SUBSTEPS):
            reach = SUBSTEPS - 1 - s
            value = {
                row: substep(value, row, [coef[row - low, i] for i in range(5)])
                for row in range(-reach, height + reach)
            }
        for row in range(height):
            final[row, g] = jnp.where(
                (place >= HALF) & (place < HALF + 3), shift(value[row], -HALF), value[row]
            )
    at_edge = (lane < 3) | (lane >= LANES - 3)
    each = chunks // parts
    size = each * GROUP * height
    copies = []
    for p in range(parts):
        for c in range(p * each, (p + 1) * each):
            which, base = base_of(c)
            for row in range(height):
                pulled = shift(final[row, which], LANES - 3 - (base + 3))
                tile[pl.ds(c * GROUP * height + row, GROUP, stride=height), :] = jnp.where(
                    at_edge, pulled, y_ref[row, pl.ds(c * GROUP, GROUP), :]
                )
        copy = pltpu.make_async_copy(
            tile.at[pl.ds(p * size, size)], out_ref.at[pl.ds(p * size, size)], sems.at[p]
        )
        copy.start()
        copies.append(copy)
    total = jnp.sum(parts_ref[...], axis=0)
    for half in range(ACOL // LANES):
        sums[:, half * LANES : (half + 1) * LANES] = total[half * tracers : (half + 1) * tracers]
    copy = pltpu.make_async_copy(sums, atmosphere_ref, sems.at[parts])
    copy.start()
    copies.append(copy)
    for copy in copies:
        copy.wait()


def remap_kernel(
    tracers,
    height,
    owners,
    owner_ref,
    surface_ref,
    cell_ref,
    column_ref,
    weight_ref,
    out_ref,
    even_ref,
    odd_ref,
    total_ref,
):
    pad = 2 * GROUP
    groups = cell_ref.shape[0] // GROUP
    total_ref[...] = jnp.zeros_like(total_ref)
    column = lax.broadcasted_iota(jnp.int32, (ACOL, LANES), 0)

    def gather(g, picked_ref):
        rows = pl.ds(g * GROUP, GROUP)
        cell = cell_ref[rows, :]
        at_lane = cell % LANES
        at_row = cell // LANES
        found = [jnp.zeros((GROUP, LANES), F32)] * tracers
        for row in range(height):
            here = at_row == row
            for k in range(tracers):
                source = jnp.broadcast_to(surface_ref[k, row : row + 1, :], (GROUP, LANES))
                found[k] = jnp.where(here, take_lanes(source, at_lane), found[k])
        weight = weight_ref[rows, :]
        for k in range(tracers):
            picked_ref[pl.ds(k, GROUP, stride=pad), :] = found[k] * weight

    def add(g, picked_ref):
        for j in range(GROUP):
            block = g * GROUP + j
            value = picked_ref[pl.ds(j * pad, pad), :]
            coarse = value.astype(jnp.bfloat16)
            fine = (value - coarse.astype(F32)).astype(jnp.bfloat16)
            chosen = (column == column_ref[pl.ds(block, 1), :]).astype(F32).astype(jnp.bfloat16)
            product = lax.dot_general(
                jnp.concatenate([coarse, fine], axis=0),
                chosen,
                (((1,), (1,)), ((), ())),
                preferred_element_type=F32,
            )
            owner = owner_ref[block]
            total_ref[owner] = total_ref[owner] + (product[:pad] + product[pad:])

    def two(i, unused):
        gather(2 * i + 1, odd_ref)
        add(2 * i, even_ref)
        gather(2 * i + 2, even_ref)
        add(2 * i + 1, odd_ref)
        return unused

    gather(0, even_ref)
    lax.fori_loop(0, groups // 2 - 1, two, 0)
    gather(groups - 1, odd_ref)
    add(groups - 2, even_ref)
    add(groups - 1, odd_ref)

    def write(o, unused):
        for half in range(ACOL // LANES):
            out_ref[o, pl.ds(half * tracers, tracers), :] = total_ref[
                o, pl.ds(0, tracers), pl.ds(half * LANES, LANES)
            ]
        return unused

    lax.fori_loop(0, owners, write, 0)


def routes(lon, lat):
    def device(i, j):
        return i * lat + j

    def swaps(first, stop):
        found = []
        for i in range(lon):
            for j in range(first, stop, 2):
                found += [(device(i, j), device(i, j + 1)), (device(i, j + 1), device(i, j))]
        return found

    fold = [(device(i, lat - 1), device(lon - 1 - i, lat - 1)) for i in range(lon)]
    for i in range(0, lon - 1, 2):
        fold += [(device(i, 0), device(i + 1, 0)), (device(i + 1, 0), device(i, 0))]
    east = [(device(i, j), device((i + 1) % lon, j)) for i in range(lon) for j in range(lat)]
    west = [(b, a) for a, b in east]
    return swaps(1, lat - 1) + fold, swaps(0, lat), east, west


def in_vmem(array):
    return pltpu.with_memory_space_constraint(array, pltpu.VMEM)


def in_hbm(array):
    return pltpu.with_memory_space_constraint(array, pltpu.HBM)


def vmem():
    return pl.BlockSpec(memory_space=pltpu.VMEM)


def smem():
    return pl.BlockSpec(memory_space=pltpu.SMEM)


def anywhere():
    return pl.BlockSpec(memory_space=pltpu.HBM)


def settings(microseconds):
    return dict(
        compiler_params=pltpu.CompilerParams(vmem_limit_bytes=16 * 1024 * 1024),
        cost_estimate=pl.CostEstimate(
            flops=0, transcendentals=0, bytes_accessed=int(microseconds * 3.5e6)
        ),
    )


def parts_of(chunks):
    return 5 if chunks % 5 == 0 else 1


def pack(height, layers, levels, flat, ocean_mask, diffusivity, remap_owner):
    chunks = layers // GROUP
    parts = parts_of(chunks)
    with jax.named_scope("pack"):
        return pl.pallas_call(
            functools.partial(pack_kernel, height, chunks, parts, levels),
            **settings(2),
            out_shape=(
                pltpu.VMEM((message_rows(layers)[1], LANES), F32),
                pltpu.VMEM((message_rows(layers)[1], LANES), F32),
                pltpu.VMEM((height * SETS * GROUP, LANES), F32),
                pltpu.VMEM((layers // levels, height, LANES), F32),
                pltpu.SMEM((remap_owner.shape[0],), jnp.int32),
            ),
            in_specs=[anywhere()] * 4,
            out_specs=(vmem(),) * 4 + (smem(),),
            scratch_shapes=[
                pltpu.VMEM(flat.shape, F32),
                pltpu.VMEM(ocean_mask.shape, ocean_mask.dtype),
                pltpu.VMEM(diffusivity.shape, F32),
                pltpu.SemaphoreType.DMA((parts + 3,)),
            ],
        )(
            in_hbm(flat),
            in_hbm(ocean_mask),
            in_hbm(diffusivity),
            in_hbm(remap_owner.reshape(-1)),
        )


def remap(owners, surface, remap_cell, remap_column, remap_weight, owner):
    tracers, height, unused = surface.shape
    with jax.named_scope("remap"):
        return pl.pallas_call(
            functools.partial(remap_kernel, tracers, height, owners),
            **settings(6),
            out_shape=pltpu.VMEM((owners, 3 * GROUP, LANES), F32),
            in_specs=[smem()] + [vmem()] * 4,
            out_specs=vmem(),
            scratch_shapes=[
                pltpu.VMEM((2 * GROUP * GROUP, LANES), F32),
                pltpu.VMEM((2 * GROUP * GROUP, LANES), F32),
                pltpu.VMEM((owners, 2 * GROUP, ACOL), F32),
            ],
        )(
            pltpu.with_memory_space_constraint(owner, pltpu.SMEM),
            in_vmem(surface),
            in_vmem(remap_cell),
            in_vmem(remap_column),
            in_vmem(remap_weight),
        )


def columns(height, layers, got_a, got_b, p):
    rows = -(-(height + 2 * (SUBSTEPS - 1)) // SLOTS) * SETS * GROUP
    with jax.named_scope("columns"):
        return pl.pallas_call(
            functools.partial(columns_kernel, height, layers // GROUP),
            **settings(1),
            out_shape=(pltpu.VMEM((rows, LANES), F32), pltpu.VMEM((rows, LANES), F32)),
            in_specs=[vmem()] * 3,
            out_specs=(vmem(), vmem()),
        )(in_vmem(got_a), in_vmem(got_b), in_vmem(p))


def tile_steps(height, layers, flat, ocean_mask, diffusivity, got_a, got_b, p):
    chunks = layers // GROUP
    parts = parts_of(chunks)
    with jax.named_scope("tile"):
        return pl.pallas_call(
            functools.partial(tile_kernel, height, chunks, parts),
            **settings(4),
            out_shape=(
                pltpu.VMEM((height, layers, LANES), F32),
                pltpu.VMEM(((height + 2 * SUBSTEPS) * SETS * GROUP, LANES), F32),
            ),
            in_specs=[anywhere()] + [vmem()] * 5,
            out_specs=(vmem(), vmem()),
            scratch_shapes=[
                pltpu.VMEM((height + 2 * (SUBSTEPS - 1), 5, GROUP, LANES), F32),
                pltpu.VMEM(flat.shape, F32),
                pltpu.SemaphoreType.DMA((parts,)),
            ],
        )(
            in_hbm(flat),
            in_vmem(ocean_mask),
            in_vmem(diffusivity),
            in_vmem(got_a),
            in_vmem(got_b),
            in_vmem(p),
        )


def edge_steps(height, layers, tracers, y, strips, from_east, from_west, sums):
    chunks = layers // GROUP
    parts = parts_of(chunks)
    with jax.named_scope("edges"):
        return pl.pallas_call(
            functools.partial(edge_kernel, height, chunks, parts, tracers),
            **settings(3),
            out_shape=(
                jax.ShapeDtypeStruct((layers * height, LANES), F32),
                jax.ShapeDtypeStruct((tracers, ACOL), F32),
            ),
            in_specs=[vmem()] * 5,
            out_specs=(anywhere(), anywhere()),
            scratch_shapes=[
                pltpu.VMEM((height + 2 * SUBSTEPS, SETS, GROUP, LANES), F32),
                pltpu.VMEM((height + 2 * (SUBSTEPS - 1), 5, GROUP, LANES), F32),
                pltpu.VMEM((height, SETS, GROUP, LANES), F32),
                pltpu.VMEM((layers * height, LANES), F32),
                pltpu.VMEM((tracers, ACOL), F32),
                pltpu.SemaphoreType.DMA((parts + 1,)),
            ],
        )(in_vmem(y), in_vmem(strips), in_vmem(from_east), in_vmem(from_west), in_vmem(sums))


def on_device(lon, lat, tracer, ocean_mask, diffusivity, remap_cell, remap_column, remap_weight, remap_owner):
    tracers, levels, height, breadth = tracer.shape
    layers = tracers * levels
    both = ("lon", "lat")
    route_a, route_b, route_east, route_west = routes(lon, lat)
    flat = tracer.reshape(layers * height, breadth)

    send_a, send_b, p, surface, owner = pack(
        height, layers, levels, flat, ocean_mask, diffusivity, remap_owner
    )
    got_a = lax.ppermute(send_a, both, route_a)
    got_b = lax.ppermute(send_b, both, route_b)

    partial = remap(lon * lat, surface, remap_cell, remap_column, remap_weight, owner)
    partial, got_a, got_b = lax.optimization_barrier((partial, got_a, got_b))
    parts = lax.all_to_all(partial, both, 0, 0, tiled=True)

    send_east, send_west = columns(height, layers, got_a, got_b, p)
    from_west = lax.ppermute(send_east, both, route_east)
    from_east = lax.ppermute(send_west, both, route_west)

    y, strips = tile_steps(height, layers, flat, ocean_mask, diffusivity, got_a, got_b, p)
    updated, atmosphere = edge_steps(
        height, layers, tracers, y, strips, from_east, from_west, parts
    )
    return updated.reshape(tracer.shape), atmosphere


def solution(mesh):
    in_specs = (
        P("member", None, "lat", "lon"),
        P("lat", "lon"),
        P("lat", "lon"),
        P(("lon", "lat"), None),
        P(("lon", "lat"), None),
        P(("lon", "lat"), None),
        P(("lon", "lat"), None),
    )
    out_specs = (P("member", None, "lat", "lon"), P("member", ("lon", "lat")))
    return jax.shard_map(
        functools.partial(on_device, mesh.shape["lon"], mesh.shape["lat"]),
        mesh=mesh,
        in_specs=in_specs,
        out_specs=out_specs,
        check_vma=False,
    )
```

```python
import functools

import jax
import jax.numpy as jnp
from jax import lax
from jax.experimental import pallas as pl
from jax.experimental.pallas import tpu as pltpu
from jax.sharding import PartitionSpec as P

ACOL = 256
SUBSTEPS = 3
LANES = 128
GROUP = 8
F32 = jnp.float32

CORNER = GROUP // 2
STRIP = 18
PER = 7
SETS = 3
HALF = 6
SLOTS = 5


def lane_iota():
    return lax.broadcasted_iota(jnp.int32, (GROUP, LANES), 1)


def shift(value, amount):
    amount = amount % LANES
    return pltpu.roll(value, amount, 1) if amount else value


def take_lanes(value, index):
    return jnp.take_along_axis(value, index, axis=1)


def is_odd():
    return lax.axis_index("lat") % 2


def register(row, which):
    return pl.ds((row * SETS + which) * GROUP, GROUP)


def base_of(chunk):
    return chunk // PER, STRIP * (chunk % PER)


def message_rows(layers):
    return SUBSTEPS * (layers + GROUP), SUBSTEPS * (layers + GROUP) + SUBSTEPS * SETS * GROUP


def pack_kernel(
    height,
    chunks,
    parts,
    levels,
    tracer_ref,
    mask_ref,
    diff_ref,
    owner_ref,
    a_ref,
    b_ref,
    p_ref,
    surface_ref,
    owners_ref,
    c_ref,
    d_ref,
    tile,
    wet_tile,
    spread_tile,
    sems,
):
    odd = jnp.full((GROUP, LANES), is_odd()) == 1
    top = (lax.axis_index("lat") == lax.axis_size("lat") - 1).astype(jnp.int32)
    each = chunks // parts
    size = each * GROUP * height
    copies = [
        pltpu.make_async_copy(
            tracer_ref.at[pl.ds(p * size, size)], tile.at[pl.ds(p * size, size)], sems.at[p]
        )
        for p in range(parts)
    ]
    copies.append(pltpu.make_async_copy(mask_ref, wet_tile, sems.at[parts]))
    copies.append(pltpu.make_async_copy(diff_ref, spread_tile, sems.at[parts + 1]))
    copies.append(pltpu.make_async_copy(owner_ref, owners_ref, sems.at[parts + 2]))
    for copy in copies:
        copy.start()

    lane = lane_iota()
    is_top = jnp.full((GROUP, LANES), top) == 1
    flip = jnp.where(is_top, LANES - 1 - lane, lane)
    stride = (chunks + 1) * GROUP
    strips_at = SUBSTEPS * stride

    def send(c, value):
        for d in range(SUBSTEPS):
            rows = pl.ds(d * stride + c * GROUP, GROUP)
            near, far = value[d], value[height - 1 - d]
            a_ref[rows, :] = take_lanes(jnp.where(odd, far, near), flip)
            b_ref[rows, :] = jnp.where(odd, near, far)

    strips = {}

    def edge(c, value):
        for row in range(height):
            add_strip(strips, row, c, value[row])

    for p in range(parts):
        copies[p].wait()
        for c in range(p * each, (p + 1) * each):
            value = {}
            for row in range(height):
                value[row] = tile[pl.ds(c * GROUP * height + row, GROUP, stride=height), :]
            send(c, value)
            edge(c, value)

    for k in range(chunks * GROUP // levels):
        surface_ref[k] = tile[pl.ds(k * levels * height, height), :]
    copies[parts].wait()
    copies[parts + 1].wait()
    copies[parts + 2].wait()
    sub = lax.broadcasted_iota(jnp.int32, (GROUP, LANES), 0)
    value = {}
    for row in range(height):
        wet = jnp.broadcast_to(wet_tile[row : row + 1, :].astype(F32), (GROUP, LANES))
        spread = jnp.broadcast_to(spread_tile[row : row + 1, :], (GROUP, LANES))
        value[row] = jnp.where(sub == 0, wet, jnp.where(sub == 1, spread, 0.0))
    send(chunks, value)
    edge(chunks, value)

    zero = jnp.zeros((GROUP, LANES), F32)
    for row in range(height):
        for g in range(SETS):
            p_ref[register(row, g), :] = strips.get((row, g), zero)
    for d in range(SUBSTEPS):
        for g in range(SETS):
            near, far = strips.get((d, g), zero), strips.get((height - 1 - d, g), zero)
            rows = pl.ds(strips_at + (d * SETS + g) * GROUP, GROUP)
            b_ref[rows, :] = jnp.where(odd, near, far)
    pack_columns(height, strips, c_ref, d_ref)


def add_strip(strips, row, chunk, value):
    which, base = base_of(chunk)
    lane = lane_iota()
    here = (lane >= base) & (lane < base + 2 * HALF)
    before = strips.get((row, which), jnp.zeros((GROUP, LANES), F32))
    strips[row, which] = jnp.where(here, shift(value, base + HALF), before)


def pack_columns(height, strips, c_ref, d_ref):
    place = lane_iota() % STRIP
    for block in range(-(-height // SLOTS)):
        for g in range(SETS):
            east = west = jnp.zeros((GROUP, LANES), F32)
            for i in range(min(SLOTS, height - SLOTS * block)):
                value = strips[SLOTS * block + i, g]
                here = (place >= 3 * i) & (place < 3 * i + 3)
                after = (place >= 3 * i + 3) & (place < 3 * i + 6)
                east = jnp.where(after, shift(value, 3 * i), east)
                west = jnp.where(here, shift(value, 3 * i - HALF), west)
            at = register(block, g)
            swap = jnp.full((GROUP, LANES), lax.axis_index("lon") % 2) == 1
            c_ref[at, :] = jnp.where(swap, west, east)
            d_ref[at, :] = jnp.where(swap, east, west)


def corner_register(p_ref, rows, first):
    lane = lane_iota()
    place = lane % STRIP
    slot = place % HALF
    column = jnp.where(slot == 1, 1, 0)
    index = lane - place + (HALF + column if first else HALF - 1 - column)
    index = jnp.where(slot < 3, index, lane)
    found = jnp.zeros((GROUP, LANES), F32)
    for g in range(SETS):
        outer = take_lanes(p_ref[register(rows[0], g), :], index)
        inner = take_lanes(p_ref[register(rows[1], g), :], index)
        found = jnp.where(place // HALF == g, jnp.where(slot == 2, inner, outer), found)
    return found


def position():
    lon, lat = lax.axis_size("lon"), lax.axis_size("lat")
    return lon, lat, lax.axis_index("lon"), lax.axis_index("lat")


def beyond_south():
    return jnp.full((GROUP, LANES), lax.axis_index("lat")) == 0


def pick_rows(odd, a_ref, b_ref, rows):
    first = a_ref[rows, :]
    second = b_ref[rows, :]
    return jnp.where(odd, first, second), jnp.where(odd, second, first)


def own_strips(height, chunks, a_ref, b_ref, p_ref):
    odd = jnp.full((GROUP, LANES), is_odd()) == 1
    stride = (chunks + 1) * GROUP
    strips_at = SUBSTEPS * stride
    first, found = {}, {}
    for d in range(SUBSTEPS):
        for c in range(chunks + 1):
            add_strip(first, d, c, a_ref[pl.ds(d * stride + c * GROUP, GROUP), :])
    zero = jnp.zeros((GROUP, LANES), F32)
    for g in range(SETS):
        for row in range(height):
            found[row, g] = p_ref[register(row, g), :]
        for d in range(SUBSTEPS):
            one = first.get((d, g), zero)
            two = b_ref[pl.ds(strips_at + (d * SETS + g) * GROUP, GROUP), :]
            found[height + d, g] = jnp.where(odd, one, two)
            found[-1 - d, g] = jnp.where(odd, two, one)
    return found


def coupling(m, s, m_n, s_n):
    return 0.5 * (s + s_n) * m * m_n


def factors(wet, spread, rows):
    north = {
        row: coupling(wet[row], spread[row], wet[row + 1], spread[row + 1])
        for row in range(rows[0] - 1, rows[-1] + 1)
    }
    found = {}
    for row in rows:
        m, s = wet[row], spread[row]
        east = coupling(m, s, shift(m, -1), shift(s, -1))
        west = shift(east, 1)
        south = north[row - 1]
        found[row] = (1.0 - (north[row] + south + east + west), north[row], south, east, west)
    return found


def substep(value, row, weight):
    centre = value[row]
    return (
        weight[0] * centre
        + (weight[1] * value[row + 1] + weight[2] * value[row - 1])
        + (weight[3] * shift(centre, -1) + weight[4] * shift(centre, 1))
    )


def tile_kernel(
    height,
    chunks,
    parts,
    tracer_ref,
    mask_ref,
    diff_ref,
    a_ref,
    b_ref,
    p_ref,
    out_ref,
    strips_ref,
    coef,
    tile,
    sems,
):
    each = chunks // parts
    size = each * GROUP * height
    copies = [
        pltpu.make_async_copy(
            tracer_ref.at[pl.ds(p * size, size)], tile.at[pl.ds(p * size, size)], sems.at[p]
        )
        for p in range(parts)
    ]
    for copy in copies:
        copy.start()
    odd = jnp.full((GROUP, LANES), is_odd()) == 1
    stride = (chunks + 1) * GROUP
    low, high = -(SUBSTEPS - 1), height + SUBSTEPS - 1

    def wide(ref, row):
        return jnp.broadcast_to(ref[row : row + 1, :].astype(F32), (GROUP, LANES))

    wet, spread = {}, {}
    south = beyond_south()
    for row in range(height):
        wet[row] = wide(mask_ref, row)
        spread[row] = wide(diff_ref, row)
    for d in range(SUBSTEPS):
        at = d * stride + chunks * GROUP
        for held, row in ((wet, at), (spread, at + 1)):
            first, second = wide(a_ref, row), wide(b_ref, row)
            held[height + d] = jnp.where(odd, first, second)
            held[-1 - d] = jnp.where(odd, second, first)
        wet[-1 - d] = jnp.where(south, 0.0, wet[-1 - d])
    weights = factors(wet, spread, range(low, high))
    for row in range(low, high):
        for i in range(5):
            coef[row - low, i] = weights[row][i]

    def one(c):
        rows = pl.ds(c * GROUP, GROUP)
        value = {
            row: tile[pl.ds(c * (GROUP * height) + row, GROUP, stride=height), :]
            for row in range(height)
        }
        for d in range(SUBSTEPS):
            value[height + d], value[-1 - d] = pick_rows(
                odd, a_ref, b_ref, pl.ds(d * stride + c * GROUP, GROUP)
            )
        for s in range(SUBSTEPS):
            reach = SUBSTEPS - 1 - s
            value = {
                row: substep(value, row, [coef[row - low, i] for i in range(5)])
                for row in range(-reach, height + reach)
            }
        for row in range(height):
            out_ref[row, rows, :] = value[row]

    def pair(i, unused):
        one(2 * i)
        one(2 * i + 1)
        return unused

    place = lane_iota() % STRIP
    for (row, g), own in own_strips(height, chunks, a_ref, b_ref, p_ref).items():
        strips_ref[register(row + SUBSTEPS, g), :] = jnp.where(
            place >= 2 * HALF, shift(own, HALF), own
        )
    for p in range(parts):
        copies[p].wait()
        lax.fori_loop(p * each // 2, (p + 1) * each // 2, pair, 0)


def edge_kernel(
    height,
    chunks,
    parts,
    tracers,
    y_ref,
    strips_ref,
    got_c_ref,
    got_d_ref,
    parts_ref,
    out_ref,
    atmosphere_ref,
    strip,
    coef,
    final,
    tile,
    sums,
    unfold,
    sems,
):
    lane = lane_iota()
    place = lane % STRIP
    low, high = -(SUBSTEPS - 1), height + SUBSTEPS - 1
    lon, lat, i_lon, i_lat = position()
    at_top = i_lat == lat - 1
    upper, lower = jnp.minimum(i_lat + 1, lat - 1), jnp.maximum(i_lat - 1, 0)
    north_east = jnp.where(at_top, (2 * lon - 2 - i_lon) % lon, (i_lon + 1) % lon) * lat + upper
    north_west = jnp.where(at_top, (lon - i_lon) % lon, (i_lon + lon - 1) % lon) * lat + upper
    south_east = (i_lon + 1) % lon * lat + lower
    south_west = (i_lon + lon - 1) % lon * lat + lower
    sub = lax.broadcasted_iota(jnp.int32, (GROUP, LANES), 0)
    carried = tracers * ACOL // LANES

    def corner(source, slot):
        folded = parts_ref[source, pl.ds(carried, CORNER), :]
        unfold[slot, 0:CORNER, :] = folded
        unfold[slot, CORNER:GROUP, :] = folded
        both = unfold[slot]
        return jnp.where(sub < CORNER, both, shift(both, -3))

    def corners(east, west, slot):
        one, two = corner(east, slot), corner(west, slot + 1)
        return jnp.where(place % HALF < 3, one, shift(two, 3))

    beyond = {
        "north": corners(north_east, north_west, 0),
        "south": corners(south_east, south_west, 2),
    }

    def at_corner(side, d, g):
        index = lane - place + HALF * g
        if d == 0:
            index = index + jnp.where(place < 9, place - HALF, 3 + 2 * HALF - 1 - place)
        else:
            index = index + jnp.where(place < 9, 2, 5)
        return take_lanes(beyond[side], jnp.clip(index, 0, LANES - 1))

    def with_halo(row, g):
        own = strips_ref[register(row + SUBSTEPS, g), :]
        if not low <= row < high:
            return own
        if row < 0:
            halo = at_corner("south", -1 - row, g)
        elif row >= height:
            halo = at_corner("north", row - height, g)
        else:
            i, rows = row % SLOTS, register(row // SLOTS, g)
            swap = jnp.full((GROUP, LANES), i_lon % 2) == 1
            from_east = jnp.where(swap, got_d_ref[rows, :], got_c_ref[rows, :])
            from_west = jnp.where(swap, got_c_ref[rows, :], got_d_ref[rows, :])
            halo = jnp.where(place < 3 * i + 3, from_east, from_west)
            halo = shift(halo, HALF - 3 * i)
        return jnp.where((place >= HALF) & (place < 2 * HALF), halo, own)

    which, base = base_of(chunks)
    wet, spread = {}, {}
    for row in range(-SUBSTEPS, height + SUBSTEPS):
        value = with_halo(row, which)
        strip[row + SUBSTEPS, which] = value
        for held, i in ((wet, 0), (spread, 1)):
            held[row] = take_lanes(
                jnp.broadcast_to(value[i : i + 1, :], (GROUP, LANES)), base + place
            )
        if row < 0:
            wet[row] = jnp.where(beyond_south(), 0.0, wet[row])
    weights = factors(wet, spread, range(low, high))
    for row in range(low, high):
        for i in range(5):
            coef[row - low, i] = weights[row][i]
    for g in range(SETS):
        value = {}
        for row in range(-SUBSTEPS, height + SUBSTEPS):
            value[row] = strip[row + SUBSTEPS, g] if g == which else with_halo(row, g)
        for s in range(SUBSTEPS):
            reach = SUBSTEPS - 1 - s
            value = {
                row: substep(value, row, [coef[row - low, i] for i in range(5)])
                for row in range(-reach, height + reach)
            }
        for row in range(height):
            final[row, g] = jnp.where(
                (place >= HALF) & (place < HALF + 3), shift(value[row], -HALF), value[row]
            )
    at_edge = (lane < 3) | (lane >= LANES - 3)
    each = chunks // parts
    size = each * GROUP * height
    copies = []
    for p in range(parts):
        for c in range(p * each, (p + 1) * each):
            which, base = base_of(c)
            for row in range(height):
                pulled = shift(final[row, which], LANES - 3 - (base + 3))
                tile[pl.ds(c * GROUP * height + row, GROUP, stride=height), :] = jnp.where(
                    at_edge, pulled, y_ref[row, pl.ds(c * GROUP, GROUP), :]
                )
        copy = pltpu.make_async_copy(
            tile.at[pl.ds(p * size, size)], out_ref.at[pl.ds(p * size, size)], sems.at[p]
        )
        copy.start()
        copies.append(copy)
    total = jnp.sum(parts_ref[...], axis=0)
    for half in range(ACOL // LANES):
        sums[:, half * LANES : (half + 1) * LANES] = total[half * tracers : (half + 1) * tracers]
    copy = pltpu.make_async_copy(sums, atmosphere_ref, sems.at[parts])
    copy.start()
    copies.append(copy)
    for copy in copies:
        copy.wait()


def remap_kernel(
    tracers,
    height,
    owners,
    owner_ref,
    surface_ref,
    cell_ref,
    column_ref,
    weight_ref,
    p_ref,
    out_ref,
    even_ref,
    odd_ref,
    total_ref,
    corner_ref,
    fold,
):
    pad = 2 * GROUP
    groups = cell_ref.shape[0] // GROUP
    total_ref[...] = jnp.zeros_like(total_ref)
    column = lax.broadcasted_iota(jnp.int32, (ACOL, LANES), 0)

    def gather(g, picked_ref):
        rows = pl.ds(g * GROUP, GROUP)
        cell = cell_ref[rows, :]
        at_lane = cell % LANES
        at_row = cell // LANES
        found = [jnp.zeros((GROUP, LANES), F32)] * tracers
        for row in range(height):
            here = at_row == row
            for k in range(tracers):
                source = jnp.broadcast_to(surface_ref[k, row : row + 1, :], (GROUP, LANES))
                found[k] = jnp.where(here, take_lanes(source, at_lane), found[k])
        weight = weight_ref[rows, :]
        for k in range(tracers):
            picked_ref[pl.ds(k, GROUP, stride=pad), :] = found[k] * weight

    def add(g, picked_ref):
        for j in range(GROUP):
            block = g * GROUP + j
            value = picked_ref[pl.ds(j * pad, pad), :]
            coarse = value.astype(jnp.bfloat16)
            fine = (value - coarse.astype(F32)).astype(jnp.bfloat16)
            chosen = (column == column_ref[pl.ds(block, 1), :]).astype(F32).astype(jnp.bfloat16)
            product = lax.dot_general(
                jnp.concatenate([coarse, fine], axis=0),
                chosen,
                (((1,), (1,)), ((), ())),
                preferred_element_type=F32,
            )
            owner = owner_ref[block]
            total_ref[owner] = total_ref[owner] + (product[:pad] + product[pad:])

    def two(i, unused):
        gather(2 * i + 1, odd_ref)
        add(2 * i, even_ref)
        gather(2 * i + 2, even_ref)
        add(2 * i + 1, odd_ref)
        return unused

    gather(0, even_ref)
    lax.fori_loop(0, groups // 2 - 1, two, 0)
    gather(groups - 1, odd_ref)
    add(groups - 2, even_ref)
    add(groups - 1, odd_ref)

    slot = lane_iota() % HALF
    for which in range(4):
        rows = (height - 1, height - 2) if which >= 2 else (0, 1)
        found = corner_register(p_ref, rows, which % 2 == 0)
        fold[which, 0:GROUP, :] = found
        fold[which, GROUP : 2 * GROUP, :] = shift(found, 3)
        corner_ref[which] = jnp.where(
            slot[:CORNER] < 3, fold[which, 0:CORNER, :], fold[which, GROUP + CORNER : 2 * GROUP, :]
        )
    lon, lat, i_lon, i_lat = position()

    def corner_for(o):
        to_lon, to_lat = lax.div(o, lat), lax.rem(o, lat)
        after = (i_lon + 1) % lon
        row = jnp.where(to_lat == i_lat + 1, 2, 0)
        which = row + jnp.where(to_lon == after, 1, 0)
        fold_which = jnp.where(to_lon == (2 * lon - 2 - i_lon) % lon, 3, 2)
        across = (i_lat == lat - 1) & (to_lat == lat - 1)
        return jnp.where(across, fold_which, which)

    carried = tracers * ACOL // LANES

    def write(o, unused):
        out_ref[o, pl.ds(carried, CORNER), :] = corner_ref[corner_for(o)]
        for half in range(ACOL // LANES):
            out_ref[o, pl.ds(half * tracers, tracers), :] = total_ref[
                o, pl.ds(0, tracers), pl.ds(half * LANES, LANES)
            ]
        return unused

    lax.fori_loop(0, owners, write, 0)


def routes(lon, lat):
    def device(i, j):
        return i * lat + j

    def swaps(first, stop):
        found = []
        for i in range(lon):
            for j in range(first, stop, 2):
                found += [(device(i, j), device(i, j + 1)), (device(i, j + 1), device(i, j))]
        return found

    fold = [(device(i, lat - 1), device(lon - 1 - i, lat - 1)) for i in range(lon)]
    for i in range(0, lon - 1, 2):
        fold += [(device(i, 0), device(i + 1, 0)), (device(i + 1, 0), device(i, 0))]
    east, west = [], []
    for i in range(0, lon, 2):
        for j in range(lat):
            one, two, three = device(i, j), device(i + 1, j), device((i + 2) % lon, j)
            east += [(one, two), (two, one)]
            west += [(two, three), (three, two)]
    return swaps(1, lat - 1) + fold, swaps(0, lat), east, west


def in_vmem(array):
    return pltpu.with_memory_space_constraint(array, pltpu.VMEM)


def in_hbm(array):
    return pltpu.with_memory_space_constraint(array, pltpu.HBM)


def vmem():
    return pl.BlockSpec(memory_space=pltpu.VMEM)


def smem():
    return pl.BlockSpec(memory_space=pltpu.SMEM)


def anywhere():
    return pl.BlockSpec(memory_space=pltpu.HBM)


def settings(microseconds):
    return dict(
        compiler_params=pltpu.CompilerParams(vmem_limit_bytes=16 * 1024 * 1024),
        cost_estimate=pl.CostEstimate(
            flops=0, transcendentals=0, bytes_accessed=int(microseconds * 3.5e6)
        ),
    )


def parts_of(chunks):
    return 5 if chunks % 5 == 0 else 1


def pack(height, layers, levels, flat, ocean_mask, diffusivity, remap_owner):
    chunks = layers // GROUP
    parts = parts_of(chunks)
    columns = -(-height // SLOTS) * SETS * GROUP
    with jax.named_scope("pack"):
        return pl.pallas_call(
            functools.partial(pack_kernel, height, chunks, parts, levels),
            **settings(2),
            out_shape=(
                pltpu.VMEM((message_rows(layers)[0], LANES), F32),
                pltpu.VMEM((message_rows(layers)[1], LANES), F32),
                pltpu.VMEM((height * SETS * GROUP, LANES), F32),
                pltpu.VMEM((layers // levels, height, LANES), F32),
                pltpu.SMEM((remap_owner.shape[0],), jnp.int32),
                pltpu.VMEM((columns, LANES), F32),
                pltpu.VMEM((columns, LANES), F32),
            ),
            in_specs=[anywhere()] * 4,
            out_specs=(vmem(),) * 4 + (smem(), vmem(), vmem()),
            scratch_shapes=[
                pltpu.VMEM(flat.shape, F32),
                pltpu.VMEM(ocean_mask.shape, ocean_mask.dtype),
                pltpu.VMEM(diffusivity.shape, F32),
                pltpu.SemaphoreType.DMA((parts + 3,)),
            ],
        )(
            in_hbm(flat),
            in_hbm(ocean_mask),
            in_hbm(diffusivity),
            in_hbm(remap_owner.reshape(-1)),
        )


def remap(owners, surface, remap_cell, remap_column, remap_weight, owner, p):
    tracers, height, unused = surface.shape
    with jax.named_scope("remap"):
        return pl.pallas_call(
            functools.partial(remap_kernel, tracers, height, owners),
            **settings(6),
            out_shape=pltpu.VMEM((owners, 3 * GROUP, LANES), F32),
            in_specs=[smem()] + [vmem()] * 5,
            out_specs=vmem(),
            scratch_shapes=[
                pltpu.VMEM((2 * GROUP * GROUP, LANES), F32),
                pltpu.VMEM((2 * GROUP * GROUP, LANES), F32),
                pltpu.VMEM((owners, 2 * GROUP, ACOL), F32),
                pltpu.VMEM((4, CORNER, LANES), F32),
                pltpu.VMEM((4, 2 * GROUP, LANES), F32),
            ],
        )(
            pltpu.with_memory_space_constraint(owner, pltpu.SMEM),
            in_vmem(surface),
            in_vmem(remap_cell),
            in_vmem(remap_column),
            in_vmem(remap_weight),
            in_vmem(p),
        )


def tile_steps(height, layers, flat, ocean_mask, diffusivity, got_a, got_b, p):
    chunks = layers // GROUP
    parts = parts_of(chunks)
    with jax.named_scope("tile"):
        return pl.pallas_call(
            functools.partial(tile_kernel, height, chunks, parts),
            **settings(4),
            out_shape=(
                pltpu.VMEM((height, layers, LANES), F32),
                pltpu.VMEM(((height + 2 * SUBSTEPS) * SETS * GROUP, LANES), F32),
            ),
            in_specs=[anywhere()] + [vmem()] * 5,
            out_specs=(vmem(), vmem()),
            scratch_shapes=[
                pltpu.VMEM((height + 2 * (SUBSTEPS - 1), 5, GROUP, LANES), F32),
                pltpu.VMEM(flat.shape, F32),
                pltpu.SemaphoreType.DMA((parts,)),
            ],
        )(
            in_hbm(flat),
            in_vmem(ocean_mask),
            in_vmem(diffusivity),
            in_vmem(got_a),
            in_vmem(got_b),
            in_vmem(p),
        )


def edge_steps(height, layers, tracers, y, strips, got_c, got_d, sums):
    chunks = layers // GROUP
    parts = parts_of(chunks)
    with jax.named_scope("edges"):
        return pl.pallas_call(
            functools.partial(edge_kernel, height, chunks, parts, tracers),
            **settings(3),
            out_shape=(
                jax.ShapeDtypeStruct((layers * height, LANES), F32),
                jax.ShapeDtypeStruct((tracers, ACOL), F32),
            ),
            in_specs=[vmem()] * 5,
            out_specs=(anywhere(), anywhere()),
            scratch_shapes=[
                pltpu.VMEM((height + 2 * SUBSTEPS, SETS, GROUP, LANES), F32),
                pltpu.VMEM((height + 2 * (SUBSTEPS - 1), 5, GROUP, LANES), F32),
                pltpu.VMEM((height, SETS, GROUP, LANES), F32),
                pltpu.VMEM((layers * height, LANES), F32),
                pltpu.VMEM((tracers, ACOL), F32),
                pltpu.VMEM((4, GROUP, LANES), F32),
                pltpu.SemaphoreType.DMA((parts + 1,)),
            ],
        )(in_vmem(y), in_vmem(strips), in_vmem(got_c), in_vmem(got_d), in_vmem(sums))


def on_device(lon, lat, tracer, ocean_mask, diffusivity, remap_cell, remap_column, remap_weight, remap_owner):
    tracers, levels, height, breadth = tracer.shape
    layers = tracers * levels
    both = ("lon", "lat")
    route_a, route_b, route_c, route_d = routes(lon, lat)
    flat = tracer.reshape(layers * height, breadth)

    send_a, send_b, p, surface, owner, send_c, send_d = pack(
        height, layers, levels, flat, ocean_mask, diffusivity, remap_owner
    )
    got_a = lax.ppermute(send_a, both, route_a)
    got_b = lax.ppermute(send_b, both, route_b)
    got_c = lax.ppermute(send_c, both, route_c)
    got_d = lax.ppermute(send_d, both, route_d)

    partial = remap(lon * lat, surface, remap_cell, remap_column, remap_weight, owner, p)
    partial, got_a, got_b, got_c = lax.optimization_barrier((partial, got_a, got_b, got_c))
    parts = lax.all_to_all(partial, both, 0, 0, tiled=True)

    y, strips = tile_steps(height, layers, flat, ocean_mask, diffusivity, got_a, got_b, p)
    updated, atmosphere = edge_steps(
        height, layers, tracers, y, strips, got_c, got_d, parts
    )
    return updated.reshape(tracer.shape), atmosphere


def solution(mesh):
    in_specs = (
        P("member", None, "lat", "lon"),
        P("lat", "lon"),
        P("lat", "lon"),
        P(("lon", "lat"), None),
        P(("lon", "lat"), None),
        P(("lon", "lat"), None),
        P(("lon", "lat"), None),
    )
    out_specs = (P("member", None, "lat", "lon"), P("member", ("lon", "lat")))
    return jax.shard_map(
        functools.partial(on_device, mesh.shape["lon"], mesh.shape["lat"]),
        mesh=mesh,
        in_specs=in_specs,
        out_specs=out_specs,
        check_vma=False,
    )
```

```python
import functools

import jax
import jax.numpy as jnp
from jax import lax
from jax.experimental import pallas as pl
from jax.experimental.pallas import tpu as pltpu
from jax.sharding import PartitionSpec as P

ACOL = 256
SUBSTEPS = 3
LANES = 128
GROUP = 8
F32 = jnp.float32

CORNER = GROUP // 2
STRIP = 18
PER = 7
SETS = 3
HALF = 6
SLOTS = 5


def lane_iota():
    return lax.broadcasted_iota(jnp.int32, (GROUP, LANES), 1)


def shift(value, amount):
    amount = amount % LANES
    return pltpu.roll(value, amount, 1) if amount else value


def take_lanes(value, index):
    return jnp.take_along_axis(value, index, axis=1)


def is_odd():
    return lax.axis_index("lat") % 2


def register(row, which):
    return pl.ds((row * SETS + which) * GROUP, GROUP)


def base_of(chunk):
    return chunk // PER, STRIP * (chunk % PER)


def message_rows(layers):
    return SUBSTEPS * (layers + GROUP), SUBSTEPS * (layers + GROUP) + SUBSTEPS * SETS * GROUP


def pack_kernel(
    height,
    chunks,
    cuts,
    levels,
    tracer_ref,
    mask_ref,
    diff_ref,
    owner_ref,
    a_ref,
    b_ref,
    p_ref,
    surface_ref,
    owners_ref,
    c_ref,
    d_ref,
    tile,
    wet_tile,
    spread_tile,
    sems,
):
    odd = jnp.full((GROUP, LANES), is_odd()) == 1
    top = (lax.axis_index("lat") == lax.axis_size("lat") - 1).astype(jnp.int32)
    parts = len(cuts) - 1
    copies = []
    for p in range(parts):
        rows = pl.ds(cuts[p] * GROUP * height, (cuts[p + 1] - cuts[p]) * GROUP * height)
        copies.append(pltpu.make_async_copy(tracer_ref.at[rows], tile.at[rows], sems.at[p]))
    copies.append(pltpu.make_async_copy(mask_ref, wet_tile, sems.at[parts]))
    copies.append(pltpu.make_async_copy(diff_ref, spread_tile, sems.at[parts + 1]))
    copies.append(pltpu.make_async_copy(owner_ref, owners_ref, sems.at[parts + 2]))
    for copy in copies:
        copy.start()

    lane = lane_iota()
    is_top = jnp.full((GROUP, LANES), top) == 1
    flip = jnp.where(is_top, LANES - 1 - lane, lane)
    stride = (chunks + 1) * GROUP
    strips_at = SUBSTEPS * stride

    def send(c, value):
        for d in range(SUBSTEPS):
            rows = pl.ds(d * stride + c * GROUP, GROUP)
            near, far = value[d], value[height - 1 - d]
            a_ref[rows, :] = take_lanes(jnp.where(odd, far, near), flip)
            b_ref[rows, :] = jnp.where(odd, near, far)

    strips = {}

    def edge(c, value):
        for row in range(height):
            add_strip(strips, row, c, value[row])

    for p in range(parts):
        copies[p].wait()
        for c in range(cuts[p], cuts[p + 1]):
            value = {}
            for row in range(height):
                value[row] = tile[pl.ds(c * GROUP * height + row, GROUP, stride=height), :]
            send(c, value)
            edge(c, value)

    for k in range(chunks * GROUP // levels):
        surface_ref[k] = tile[pl.ds(k * levels * height, height), :]
    copies[parts].wait()
    copies[parts + 1].wait()
    copies[parts + 2].wait()
    sub = lax.broadcasted_iota(jnp.int32, (GROUP, LANES), 0)
    value = {}
    for row in range(height):
        wet = jnp.broadcast_to(wet_tile[row : row + 1, :].astype(F32), (GROUP, LANES))
        spread = jnp.broadcast_to(spread_tile[row : row + 1, :], (GROUP, LANES))
        value[row] = jnp.where(sub == 0, wet, jnp.where(sub == 1, spread, 0.0))
    send(chunks, value)
    edge(chunks, value)

    zero = jnp.zeros((GROUP, LANES), F32)
    for row in range(height):
        for g in range(SETS):
            p_ref[register(row, g), :] = strips.get((row, g), zero)
    pack_columns(height, strips, c_ref, d_ref)


def add_strip(strips, row, chunk, value):
    which, base = base_of(chunk)
    lane = lane_iota()
    here = (lane >= base) & (lane < base + 2 * HALF)
    before = strips.get((row, which), jnp.zeros((GROUP, LANES), F32))
    strips[row, which] = jnp.where(here, shift(value, base + HALF), before)


def pack_columns(height, strips, c_ref, d_ref):
    place = lane_iota() % STRIP
    for block in range(-(-height // SLOTS)):
        for g in range(SETS):
            east = west = jnp.zeros((GROUP, LANES), F32)
            for i in range(min(SLOTS, height - SLOTS * block)):
                value = strips[SLOTS * block + i, g]
                here = (place >= 3 * i) & (place < 3 * i + 3)
                after = (place >= 3 * i + 3) & (place < 3 * i + 6)
                east = jnp.where(after, shift(value, 3 * i), east)
                west = jnp.where(here, shift(value, 3 * i - HALF), west)
            at = register(block, g)
            swap = jnp.full((GROUP, LANES), lax.axis_index("lon") % 2) == 1
            c_ref[at, :] = jnp.where(swap, west, east)
            d_ref[at, :] = jnp.where(swap, east, west)


def corner_register(p_ref, rows, first):
    lane = lane_iota()
    place = lane % STRIP
    slot = place % HALF
    column = jnp.where(slot == 1, 1, 0)
    index = lane - place + (HALF + column if first else HALF - 1 - column)
    index = jnp.clip(jnp.where(slot < 3, index, lane), 0, LANES - 1)
    found = jnp.zeros((GROUP, LANES), F32)
    for g in range(SETS):
        outer = take_lanes(p_ref[register(rows[0], g), :], index)
        inner = take_lanes(p_ref[register(rows[1], g), :], index)
        found = jnp.where(place // HALF == g, jnp.where(slot == 2, inner, outer), found)
    return found


def position():
    lon, lat = lax.axis_size("lon"), lax.axis_size("lat")
    return lon, lat, lax.axis_index("lon"), lax.axis_index("lat")


def beyond_south():
    return jnp.full((GROUP, LANES), lax.axis_index("lat")) == 0


def pick_rows(odd, a_ref, b_ref, rows):
    first = a_ref[rows, :]
    second = b_ref[rows, :]
    return jnp.where(odd, first, second), jnp.where(odd, second, first)


def own_strips(height, chunks, a_ref, b_ref, p_ref):
    odd = jnp.full((GROUP, LANES), is_odd()) == 1
    stride = (chunks + 1) * GROUP
    strips_at = SUBSTEPS * stride
    first, second, found = {}, {}, {}
    for d in range(SUBSTEPS):
        for c in range(chunks + 1):
            add_strip(first, d, c, a_ref[pl.ds(d * stride + c * GROUP, GROUP), :])
            add_strip(second, d, c, b_ref[pl.ds(d * stride + c * GROUP, GROUP), :])
    zero = jnp.zeros((GROUP, LANES), F32)
    for g in range(SETS):
        for row in range(height):
            found[row, g] = p_ref[register(row, g), :]
        for d in range(SUBSTEPS):
            one, two = first.get((d, g), zero), second.get((d, g), zero)
            found[height + d, g] = jnp.where(odd, one, two)
            found[-1 - d, g] = jnp.where(odd, two, one)
    return found


def coupling(m, s, m_n, s_n):
    return 0.5 * (s + s_n) * m * m_n


def factors(wet, spread, rows):
    north = {
        row: coupling(wet[row], spread[row], wet[row + 1], spread[row + 1])
        for row in range(rows[0] - 1, rows[-1] + 1)
    }
    found = {}
    for row in rows:
        m, s = wet[row], spread[row]
        east = coupling(m, s, shift(m, -1), shift(s, -1))
        west = shift(east, 1)
        south = north[row - 1]
        found[row] = (1.0 - (north[row] + south + east + west), north[row], south, east, west)
    return found


def substep(value, row, weight):
    centre = value[row]
    return (
        weight[0] * centre
        + (weight[1] * value[row + 1] + weight[2] * value[row - 1])
        + (weight[3] * shift(centre, -1) + weight[4] * shift(centre, 1))
    )


def tile_kernel(
    height,
    chunks,
    parts,
    tracer_ref,
    mask_ref,
    diff_ref,
    a_ref,
    b_ref,
    p_ref,
    out_ref,
    strips_ref,
    coef,
    tile,
    sems,
):
    each = chunks // parts
    size = each * GROUP * height
    copies = [
        pltpu.make_async_copy(
            tracer_ref.at[pl.ds(p * size, size)], tile.at[pl.ds(p * size, size)], sems.at[p]
        )
        for p in range(parts)
    ]
    for copy in copies:
        copy.start()
    odd = jnp.full((GROUP, LANES), is_odd()) == 1
    stride = (chunks + 1) * GROUP
    low, high = -(SUBSTEPS - 1), height + SUBSTEPS - 1

    def wide(ref, row):
        return jnp.broadcast_to(ref[row : row + 1, :].astype(F32), (GROUP, LANES))

    wet, spread = {}, {}
    south = beyond_south()
    for row in range(height):
        wet[row] = wide(mask_ref, row)
        spread[row] = wide(diff_ref, row)
    for d in range(SUBSTEPS):
        at = d * stride + chunks * GROUP
        for held, row in ((wet, at), (spread, at + 1)):
            first, second = wide(a_ref, row), wide(b_ref, row)
            held[height + d] = jnp.where(odd, first, second)
            held[-1 - d] = jnp.where(odd, second, first)
        wet[-1 - d] = jnp.where(south, 0.0, wet[-1 - d])
    weights = factors(wet, spread, range(low, high))
    for row in range(low, high):
        for i in range(5):
            coef[row - low, i] = weights[row][i]

    def one(c):
        rows = pl.ds(c * GROUP, GROUP)
        value = {
            row: tile[pl.ds(c * (GROUP * height) + row, GROUP, stride=height), :]
            for row in range(height)
        }
        for d in range(SUBSTEPS):
            value[height + d], value[-1 - d] = pick_rows(
                odd, a_ref, b_ref, pl.ds(d * stride + c * GROUP, GROUP)
            )
        for s in range(SUBSTEPS):
            reach = SUBSTEPS - 1 - s
            value = {
                row: substep(value, row, [coef[row - low, i] for i in range(5)])
                for row in range(-reach, height + reach)
            }
        for row in range(height):
            out_ref[row, rows, :] = value[row]

    def pair(i, unused):
        one(2 * i)
        one(2 * i + 1)
        return unused

    place = lane_iota() % STRIP
    for (row, g), own in own_strips(height, chunks, a_ref, b_ref, p_ref).items():
        strips_ref[register(row + SUBSTEPS, g), :] = jnp.where(
            place >= 2 * HALF, shift(own, HALF), own
        )
    for p in range(parts):
        copies[p].wait()
        lax.fori_loop(p * each // 2, (p + 1) * each // 2, pair, 0)


def edge_kernel(
    height,
    chunks,
    parts,
    tracers,
    y_ref,
    strips_ref,
    got_c_ref,
    got_d_ref,
    parts_ref,
    out_ref,
    atmosphere_ref,
    strip,
    coef,
    final,
    tile,
    sums,
    unfold,
    sems,
):
    lane = lane_iota()
    place = lane % STRIP
    low, high = -(SUBSTEPS - 1), height + SUBSTEPS - 1
    lon, lat, i_lon, i_lat = position()
    at_top = i_lat == lat - 1
    upper, lower = jnp.minimum(i_lat + 1, lat - 1), jnp.maximum(i_lat - 1, 0)
    north_east = jnp.where(at_top, (2 * lon - 2 - i_lon) % lon, (i_lon + 1) % lon) * lat + upper
    north_west = jnp.where(at_top, (lon - i_lon) % lon, (i_lon + lon - 1) % lon) * lat + upper
    south_east = (i_lon + 1) % lon * lat + lower
    south_west = (i_lon + lon - 1) % lon * lat + lower
    sub = lax.broadcasted_iota(jnp.int32, (GROUP, LANES), 0)
    carried = 2 * GROUP + CORNER

    def corner(source, slot):
        folded = parts_ref[source, pl.ds(carried, CORNER), :]
        unfold[slot, 0:CORNER, :] = folded
        unfold[slot, CORNER:GROUP, :] = folded
        both = unfold[slot]
        return jnp.where(sub < CORNER, both, shift(both, -3))

    def corners(east, west, slot):
        one, two = corner(east, slot), corner(west, slot + 1)
        return jnp.where(place % HALF < 3, one, shift(two, 3))

    beyond = {
        "north": corners(north_east, north_west, 0),
        "south": corners(south_east, south_west, 2),
    }

    def at_corner(side, d, g):
        index = lane - place + HALF * g
        if d == 0:
            index = index + jnp.where(place < 9, place - HALF, 3 + 2 * HALF - 1 - place)
        else:
            index = index + jnp.where(place < 9, 2, 5)
        return take_lanes(beyond[side], jnp.clip(index, 0, LANES - 1))

    def with_halo(row, g):
        own = strips_ref[register(row + SUBSTEPS, g), :]
        if not low <= row < high:
            return own
        if row < 0:
            halo = at_corner("south", -1 - row, g)
        elif row >= height:
            halo = at_corner("north", row - height, g)
        else:
            i, rows = row % SLOTS, register(row // SLOTS, g)
            swap = jnp.full((GROUP, LANES), i_lon % 2) == 1
            from_east = jnp.where(swap, got_d_ref[rows, :], got_c_ref[rows, :])
            from_west = jnp.where(swap, got_c_ref[rows, :], got_d_ref[rows, :])
            halo = jnp.where(place < 3 * i + 3, from_east, from_west)
            halo = shift(halo, HALF - 3 * i)
        return jnp.where((place >= HALF) & (place < 2 * HALF), halo, own)

    which, base = base_of(chunks)
    wet, spread = {}, {}
    for row in range(-SUBSTEPS, height + SUBSTEPS):
        value = with_halo(row, which)
        strip[row + SUBSTEPS, which] = value
        for held, i in ((wet, 0), (spread, 1)):
            held[row] = take_lanes(
                jnp.broadcast_to(value[i : i + 1, :], (GROUP, LANES)), base + place
            )
        if row < 0:
            wet[row] = jnp.where(beyond_south(), 0.0, wet[row])
    weights = factors(wet, spread, range(low, high))
    for row in range(low, high):
        for i in range(5):
            coef[row - low, i] = weights[row][i]
    for g in range(SETS):
        value = {}
        for row in range(-SUBSTEPS, height + SUBSTEPS):
            value[row] = strip[row + SUBSTEPS, g] if g == which else with_halo(row, g)
        for s in range(SUBSTEPS):
            reach = SUBSTEPS - 1 - s
            value = {
                row: substep(value, row, [coef[row - low, i] for i in range(5)])
                for row in range(-reach, height + reach)
            }
        for row in range(height):
            final[row, g] = jnp.where(
                (place >= HALF) & (place < HALF + 3), shift(value[row], -HALF), value[row]
            )
    at_edge = (lane < 3) | (lane >= LANES - 3)
    each = chunks // parts
    size = each * GROUP * height
    copies = []
    for p in range(parts):
        for c in range(p * each, (p + 1) * each):
            which, base = base_of(c)
            for row in range(height):
                pulled = shift(final[row, which], LANES - 3 - (base + 3))
                tile[pl.ds(c * GROUP * height + row, GROUP, stride=height), :] = jnp.where(
                    at_edge, pulled, y_ref[row, pl.ds(c * GROUP, GROUP), :]
                )
        copy = pltpu.make_async_copy(
            tile.at[pl.ds(p * size, size)], out_ref.at[pl.ds(p * size, size)], sems.at[p]
        )
        copy.start()
        copies.append(copy)
    total = jnp.sum(parts_ref[...], axis=0)
    rest = tracers - GROUP
    for half in range(ACOL // LANES):
        lanes = slice(half * LANES, (half + 1) * LANES)
        sums[0:GROUP, lanes] = total[half * GROUP : (half + 1) * GROUP]
        at = 2 * GROUP + half * rest
        sums[GROUP:tracers, lanes] = total[at : at + rest]
    copy = pltpu.make_async_copy(sums, atmosphere_ref, sems.at[parts])
    copy.start()
    copies.append(copy)
    for copy in copies:
        copy.wait()


def remap_kernel(
    tracers,
    height,
    owners,
    owner_ref,
    surface_ref,
    cell_ref,
    column_ref,
    weight_ref,
    p_ref,
    out_ref,
    even_ref,
    odd_ref,
    total_ref,
    corner_ref,
):
    pad = 2 * GROUP
    groups = cell_ref.shape[0] // GROUP
    total_ref[...] = jnp.zeros_like(total_ref)
    column = lax.broadcasted_iota(jnp.int32, (ACOL, LANES), 0).astype(jnp.bfloat16)
    one, none = jnp.ones((), jnp.bfloat16), jnp.zeros((), jnp.bfloat16)

    def gather(g, picked_ref):
        rows = pl.ds(g * GROUP, GROUP)
        cell = cell_ref[rows, :]
        at_lane = cell % LANES
        at_row = cell // LANES
        found = [jnp.zeros((GROUP, LANES), F32)] * tracers
        for row in range(height):
            here = at_row == row
            for k in range(tracers):
                source = jnp.broadcast_to(surface_ref[k, row : row + 1, :], (GROUP, LANES))
                found[k] = jnp.where(here, take_lanes(source, at_lane), found[k])
        weight = weight_ref[rows, :]
        for k in range(tracers):
            picked_ref[pl.ds(k, GROUP, stride=pad), :] = found[k] * weight

    def add(g, picked_ref):
        for j in range(GROUP):
            block = g * GROUP + j
            value = picked_ref[pl.ds(j * pad, pad), :]
            coarse = value.astype(jnp.bfloat16)
            fine = (value - coarse.astype(F32)).astype(jnp.bfloat16)
            named = column_ref[pl.ds(block, 1), :].astype(F32).astype(jnp.bfloat16)
            chosen = jnp.where(column == named, one, none)
            product = lax.dot_general(
                jnp.concatenate([coarse, fine], axis=0),
                chosen,
                (((1,), (1,)), ((), ())),
                preferred_element_type=F32,
            )
            owner = owner_ref[block]
            total_ref[owner] = total_ref[owner] + (product[:pad] + product[pad:])

    def two(i, unused):
        gather(2 * i + 1, odd_ref)
        add(2 * i, even_ref)
        gather(2 * i + 2, even_ref)
        add(2 * i + 1, odd_ref)
        return unused

    gather(0, even_ref)
    lax.fori_loop(0, groups // 2 - 1, two, 0)
    gather(groups - 1, odd_ref)
    add(groups - 2, even_ref)
    add(groups - 1, odd_ref)

    slot = lane_iota() % HALF
    for which in range(4):
        rows = (height - 1, height - 2) if which >= 2 else (0, 1)
        found = corner_register(p_ref, rows, which % 2 == 0)
        corner_ref[which] = jnp.where(slot < 3, pltpu.roll(found, CORNER, 0), shift(found, 3))
    lon, lat, i_lon, i_lat = position()

    def corner_for(o):
        to_lon, to_lat = lax.div(o, lat), lax.rem(o, lat)
        after = (i_lon + 1) % lon
        row = jnp.where(to_lat == i_lat + 1, 2, 0)
        which = row + jnp.where(to_lon == after, 1, 0)
        fold_which = jnp.where(to_lon == (2 * lon - 2 - i_lon) % lon, 3, 2)
        across = (i_lat == lat - 1) & (to_lat == lat - 1)
        return jnp.where(across, fold_which, which)

    rest = tracers - GROUP
    sub = lax.broadcasted_iota(jnp.int32, (GROUP, LANES), 0)

    def write(o, unused):
        out_ref[o, 0:GROUP, :] = total_ref[o, 0:GROUP, 0:LANES]
        out_ref[o, GROUP : 2 * GROUP, :] = total_ref[o, 0:GROUP, LANES:ACOL]
        left = total_ref[o, GROUP : 2 * GROUP, 0:LANES]
        right = pltpu.roll(total_ref[o, GROUP : 2 * GROUP, LANES:ACOL], rest, 0)
        last = jnp.where(sub < rest, left, jnp.where(sub < CORNER, right, corner_ref[corner_for(o)]))
        out_ref[o, 2 * GROUP : 3 * GROUP, :] = last
        return unused

    lax.fori_loop(0, owners, write, 0)


def routes(lon, lat):
    def device(i, j):
        return i * lat + j

    def swaps(first, stop):
        found = []
        for i in range(lon):
            for j in range(first, stop, 2):
                found += [(device(i, j), device(i, j + 1)), (device(i, j + 1), device(i, j))]
        return found

    fold = [(device(i, lat - 1), device(lon - 1 - i, lat - 1)) for i in range(lon)]
    for i in range(0, lon - 1, 2):
        fold += [(device(i, 0), device(i + 1, 0)), (device(i + 1, 0), device(i, 0))]
    east, west = [], []
    for i in range(0, lon, 2):
        for j in range(lat):
            one, two, three = device(i, j), device(i + 1, j), device((i + 2) % lon, j)
            east += [(one, two), (two, one)]
            west += [(two, three), (three, two)]
    return swaps(1, lat - 1) + fold, swaps(0, lat), east, west


def in_vmem(array):
    return pltpu.with_memory_space_constraint(array, pltpu.VMEM)


def in_hbm(array):
    return pltpu.with_memory_space_constraint(array, pltpu.HBM)


def vmem():
    return pl.BlockSpec(memory_space=pltpu.VMEM)


def smem():
    return pl.BlockSpec(memory_space=pltpu.SMEM)


def anywhere():
    return pl.BlockSpec(memory_space=pltpu.HBM)


def settings(microseconds):
    return dict(
        compiler_params=pltpu.CompilerParams(vmem_limit_bytes=16 * 1024 * 1024),
        cost_estimate=pl.CostEstimate(
            flops=0, transcendentals=0, bytes_accessed=int(microseconds * 3.5e6)
        ),
    )


def parts_of(chunks, wanted):
    return wanted if chunks % wanted == 0 else 1


def pack(height, layers, levels, flat, ocean_mask, diffusivity, remap_owner):
    chunks = layers // GROUP
    cuts = (0, chunks // 2, chunks)
    columns = -(-height // SLOTS) * SETS * GROUP
    with jax.named_scope("pack"):
        return pl.pallas_call(
            functools.partial(pack_kernel, height, chunks, cuts, levels),
            **settings(2),
            out_shape=(
                pltpu.VMEM((message_rows(layers)[0], LANES), F32),
                pltpu.VMEM((message_rows(layers)[0], LANES), F32),
                pltpu.VMEM((height * SETS * GROUP, LANES), F32),
                pltpu.VMEM((layers // levels, height, LANES), F32),
                pltpu.SMEM((remap_owner.shape[0],), jnp.int32),
                pltpu.VMEM((columns, LANES), F32),
                pltpu.VMEM((columns, LANES), F32),
            ),
            in_specs=[anywhere()] * 4,
            out_specs=(vmem(),) * 4 + (smem(), vmem(), vmem()),
            scratch_shapes=[
                pltpu.VMEM(flat.shape, F32),
                pltpu.VMEM(ocean_mask.shape, ocean_mask.dtype),
                pltpu.VMEM(diffusivity.shape, F32),
                pltpu.SemaphoreType.DMA((len(cuts) + 2,)),
            ],
        )(
            in_hbm(flat),
            in_hbm(ocean_mask),
            in_hbm(diffusivity),
            in_hbm(remap_owner.reshape(-1)),
        )


def remap(owners, surface, remap_cell, remap_column, remap_weight, owner, p):
    tracers, height, unused = surface.shape
    with jax.named_scope("remap"):
        return pl.pallas_call(
            functools.partial(remap_kernel, tracers, height, owners),
            **settings(6),
            out_shape=pltpu.VMEM((owners, 3 * GROUP, LANES), F32),
            in_specs=[smem()] + [vmem()] * 5,
            out_specs=vmem(),
            scratch_shapes=[
                pltpu.VMEM((2 * GROUP * GROUP, LANES), F32),
                pltpu.VMEM((2 * GROUP * GROUP, LANES), F32),
                pltpu.VMEM((owners, 2 * GROUP, ACOL), F32),
                pltpu.VMEM((4, GROUP, LANES), F32),
            ],
        )(
            pltpu.with_memory_space_constraint(owner, pltpu.SMEM),
            in_vmem(surface),
            in_vmem(remap_cell),
            in_vmem(remap_column),
            in_vmem(remap_weight),
            in_vmem(p),
        )


def tile_steps(height, layers, flat, ocean_mask, diffusivity, got_a, got_b, p):
    chunks = layers // GROUP
    parts = parts_of(chunks, 10)
    with jax.named_scope("tile"):
        return pl.pallas_call(
            functools.partial(tile_kernel, height, chunks, parts),
            **settings(4),
            out_shape=(
                pltpu.VMEM((height, layers, LANES), F32),
                pltpu.VMEM(((height + 2 * SUBSTEPS) * SETS * GROUP, LANES), F32),
            ),
            in_specs=[anywhere()] + [vmem()] * 5,
            out_specs=(vmem(), vmem()),
            scratch_shapes=[
                pltpu.VMEM((height + 2 * (SUBSTEPS - 1), 5, GROUP, LANES), F32),
                pltpu.VMEM(flat.shape, F32),
                pltpu.SemaphoreType.DMA((parts,)),
            ],
        )(
            in_hbm(flat),
            in_vmem(ocean_mask),
            in_vmem(diffusivity),
            in_vmem(got_a),
            in_vmem(got_b),
            in_vmem(p),
        )


def edge_steps(height, layers, tracers, y, strips, got_c, got_d, sums):
    chunks = layers // GROUP
    parts = parts_of(chunks, 5)
    with jax.named_scope("edges"):
        return pl.pallas_call(
            functools.partial(edge_kernel, height, chunks, parts, tracers),
            **settings(3),
            out_shape=(
                jax.ShapeDtypeStruct((layers * height, LANES), F32),
                jax.ShapeDtypeStruct((tracers, ACOL), F32),
            ),
            in_specs=[vmem()] * 5,
            out_specs=(anywhere(), anywhere()),
            scratch_shapes=[
                pltpu.VMEM((height + 2 * SUBSTEPS, SETS, GROUP, LANES), F32),
                pltpu.VMEM((height + 2 * (SUBSTEPS - 1), 5, GROUP, LANES), F32),
                pltpu.VMEM((height, SETS, GROUP, LANES), F32),
                pltpu.VMEM((layers * height, LANES), F32),
                pltpu.VMEM((tracers, ACOL), F32),
                pltpu.VMEM((4, GROUP, LANES), F32),
                pltpu.SemaphoreType.DMA((parts + 1,)),
            ],
        )(in_vmem(y), in_vmem(strips), in_vmem(got_c), in_vmem(got_d), in_vmem(sums))


def on_device(lon, lat, tracer, ocean_mask, diffusivity, remap_cell, remap_column, remap_weight, remap_owner):
    tracers, levels, height, breadth = tracer.shape
    layers = tracers * levels
    both = ("lon", "lat")
    route_a, route_b, route_c, route_d = routes(lon, lat)
    flat = tracer.reshape(layers * height, breadth)

    send_a, send_b, p, surface, owner, send_c, send_d = pack(
        height, layers, levels, flat, ocean_mask, diffusivity, remap_owner
    )
    got_a = lax.ppermute(send_a, both, route_a)
    got_b = lax.ppermute(send_b, both, route_b)
    got_c = lax.ppermute(send_c, both, route_c)
    got_d = lax.ppermute(send_d, both, route_d)

    partial = remap(lon * lat, surface, remap_cell, remap_column, remap_weight, owner, p)
    partial, got_a, got_b, got_c = lax.optimization_barrier((partial, got_a, got_b, got_c))
    parts = lax.all_to_all(partial, both, 0, 0, tiled=True)

    y, strips = tile_steps(height, layers, flat, ocean_mask, diffusivity, got_a, got_b, p)
    updated, atmosphere = edge_steps(
        height, layers, tracers, y, strips, got_c, got_d, parts
    )
    return updated.reshape(tracer.shape), atmosphere


def solution(mesh):
    in_specs = (
        P("member", None, "lat", "lon"),
        P("lat", "lon"),
        P("lat", "lon"),
        P(("lon", "lat"), None),
        P(("lon", "lat"), None),
        P(("lon", "lat"), None),
        P(("lon", "lat"), None),
    )
    out_specs = (P("member", None, "lat", "lon"), P("member", ("lon", "lat")))
    return jax.shard_map(
        functools.partial(on_device, mesh.shape["lon"], mesh.shape["lat"]),
        mesh=mesh,
        in_specs=in_specs,
        out_specs=out_specs,
        check_vma=False,
    )
```
